32 devices in a mesh: row: 8 (over y, x, core), col: 4 (over z).
Axes of the slice: x: 2, y: 2, z: 4, core: 2. Of those that a mesh axis runs over, the one named last changes fastest.
Arguments:
- images: bfloat16 [2, 32, 64, 2048], P(None, 'row', None, 'col'), may hold values from -6 to 6
- dw_kernel: float32 [7, 7, 2048], P(None, None, 'col'), may hold values from -3 to 3
- norm_gain: float32 [2048], P('col'), may hold values from 0.5 to 1.5
- proj_in: bfloat16 [2048, 8192], P('row', 'col'), may hold values from -0.125 to 0.125
- proj_out: bfloat16 [2048, 8192], P('row', 'col'), may hold values from -0.0625 to 0.0625
- layer_scale: float32 [2048], P('col'), may hold values from 0.1 to 1.9
- cotangent: bfloat16 [2, 32, 64, 2048], P(None, 'row', None, 'col'), may hold values from -0.59765625 to 0.59765625
Outputs:
- block_out: bfloat16 [2, 32, 64, 2048], P(None, 'row', None, 'col')
- grad_images: bfloat16 [2, 32, 64, 2048], P(None, 'row', None, 'col')
- grad_proj_in: bfloat16 [2048, 8192], P('row', 'col')
- grad_proj_out: bfloat16 [2048, 8192], P('row', 'col')
The draws below stay inside these ranges and needn't reach their ends.
All inputs are finite; a program needn't handle non-finite values.
Results may differ from the reference program's by a relative error of at most 0.023.
Values may be sent and summed in bfloat16 or wider, within the bound.
No kernel may reach another device: no remote copies, remote signals or barrier semaphores. Data moves between devices by JAX's collectives and lax.ppermute only.
A program may use at most 128 MiB of HBM per device.

```python
import jax
import jax.numpy as jnp
from jax import lax

C = 2048
HID = 8192
KS = 7
STRIP = 4
IMG_W = 64
BATCH = 2
IMG_H = 32
N_ROW = 8
N_COL = 4


def draw_dw_kernel(key, part):
    first_key, second_key = jax.random.split(key)
    channel = jnp.arange(C, dtype=jnp.float32) / max(C - 1, 1)
    jitter = jnp.exp(jax.random.uniform(second_key, (C,), jnp.float32, jnp.log(0.7), jnp.log(1.4)))
    factor = jnp.exp(jnp.log(3.0) * channel) * jitter
    taps = jax.random.truncated_normal(first_key, -3.0, 3.0, (KS, KS, C), jnp.float32) / 7.0
    return (taps * factor).astype(jnp.float32)


def raised(array, own_key, source, target, shards_of, factor):
    owner, partner = [(jnp.arange(array.shape[position]) // (array.shape[position] // shards_of)).reshape([-1 if axis == position else 1 for axis in range(array.ndim)]) for position in (source, target)]
    chosen = jax.random.permutation(own_key, shards_of)[partner]
    strong = (owner == chosen) | (owner == (partner + shards_of // 2) % shards_of)
    return jnp.where(strong, factor * array, array)


def block_levels(rng, shape, cuts, smallest, largest):
    gain = 1.0
    for dim, blocks in cuts:
        steps = jax.random.uniform(jax.random.fold_in(jax.random.fold_in(rng, 6), dim), (blocks,), jnp.float32, smallest / len(cuts), largest / len(cuts))
        gain = gain * jnp.repeat(jnp.exp(steps), shape[dim] // blocks).reshape((-1,) + (1,) * (len(shape) - 1 - dim))
    return gain


def scatter_about(stream_key, extent, scale, most, cuts=(), held_as=jnp.bfloat16):
    result = scale * jax.random.normal(stream_key, extent, jnp.float32)
    if cuts:
        result = result * block_levels(stream_key, extent, cuts, -0.22, 0.18)
    return jnp.clip(result, -most, most).astype(held_as)


def bell_draw_with(own_key, dims, deviation, most, cuts, heavy, held_as=jnp.bfloat16):
    values = deviation * jax.random.normal(own_key, dims, jnp.float32)
    if cuts:
        values = values * block_levels(own_key, dims, cuts, -0.22, 0.18)
    return jnp.clip(raised(values, jax.random.fold_in(own_key, 3), *heavy), -most, most).astype(held_as)


def setup_inputs(seed: int = 0) -> dict:
    key_of = jax.random.split(jax.random.key(seed), 8)
    return {
        "images": scatter_about(key_of[0], (BATCH, IMG_H, IMG_W, C), 1.0, 6.0, ((1, 8), (3, 4))),
        "dw_kernel": draw_dw_kernel(jax.random.fold_in(key_of[7], 71), 0),
        "norm_gain": jnp.clip(1.0 + 0.1 * jax.random.normal(key_of[2], (C,), jnp.float32), 0.5, 1.5),
        "proj_in": scatter_about(key_of[3], (C, HID), C ** -0.5, 0.125, ((0, 8), (1, 4))),
        "proj_out": scatter_about(key_of[4], (C, HID), HID ** -0.5, 0.0625, ((0, 8), (1, 4))),
        "layer_scale": jnp.clip(1.0 + 0.18 * jax.random.normal(key_of[5], (C,), jnp.float32), 0.1, 1.9),
        "cotangent": bell_draw_with(key_of[6], (BATCH, IMG_H, IMG_W, C), 0.1, 0.59765625, ((1, 8), (3, 4)), (1, 3, 8, 2.0)),
    }


def rounded(partial_sum):
    return lax.optimization_barrier(partial_sum.astype(jnp.bfloat16)).astype(jnp.float32)

def taps_sum(padded, dw_kernel, img_rows, img_cols, flipped):
    total = jnp.zeros(padded.shape[:1] + (img_rows, img_cols) + padded.shape[3:], jnp.float32)
    reach = 2 * (KS // 2)
    for tap_row in range(KS):
        for tap_col in range(KS):
            off_row = reach - tap_row if flipped else tap_row
            off_col = reach - tap_col if flipped else tap_col
            total = total + dw_kernel[tap_row, tap_col] * padded[:, off_row:off_row + img_rows, off_col:off_col + img_cols, :]
    return total

def gelu_slope(values):
    return 0.5 * (1.0 + lax.erf(values * 0.7071067811865476)) + values * jnp.exp(-0.5 * values * values) * 0.3989422804014327

def reference(images, dw_kernel, norm_gain, proj_in, proj_out, layer_scale, cotangent):
    pixels = BATCH * IMG_H * IMG_W
    reach = KS // 2
    padded = jnp.pad(images.astype(jnp.float32), ((0, 0), (reach, reach), (reach, reach), (0, 0)))
    conv_out = taps_sum(padded, dw_kernel, IMG_H, IMG_W, False).reshape(pixels, C)
    row_mean = lax.optimization_barrier(jnp.mean(conv_out, axis=1))
    centred = conv_out - row_mean[:, None]
    row_var = lax.optimization_barrier(jnp.mean(centred * centred, axis=1))
    inv_std = lax.rsqrt(row_var + 1e-06)
    normed = centred * inv_std[:, None]
    scaled = (normed * norm_gain).astype(jnp.bfloat16)
    hidden_pre = jnp.dot(scaled, proj_in, preferred_element_type=jnp.float32)
    hidden = jax.nn.gelu(hidden_pre, approximate=False).astype(jnp.bfloat16)
    hid_cols = HID // N_COL
    contract_last = (((1,), (1,)), ((), ()))
    contract_first = (((0,), (0,)), ((), ()))

    def add_branch(index, total):
        first_col = jnp.asarray(index, jnp.int32) * hid_cols
        act_block = lax.dynamic_slice_in_dim(hidden, first_col, hid_cols, 1)
        weight_block = lax.dynamic_slice_in_dim(proj_out, first_col, hid_cols, 1)
        return total + rounded(lax.dot_general(act_block, weight_block, contract_last, preferred_element_type=jnp.float32))
    branch = lax.fori_loop(0, N_COL, add_branch, jnp.zeros((pixels, C), jnp.float32))
    block_out = (images.reshape(pixels, C).astype(jnp.float32) + layer_scale * branch).astype(jnp.bfloat16)
    cot_flat = cotangent.reshape(pixels, C).astype(jnp.float32)
    grad_branch = (cot_flat * layer_scale).astype(jnp.bfloat16)
    grad_hidden = jnp.dot(grad_branch, proj_out, preferred_element_type=jnp.float32)
    grad_pre = (grad_hidden * gelu_slope(hidden_pre)).astype(jnp.bfloat16)
    strip_pix = STRIP * IMG_W
    branch_strips = grad_branch.reshape(BATCH, N_ROW, strip_pix, C)
    hidden_strips = hidden.reshape(BATCH, N_ROW, strip_pix, HID)
    scaled_strips = scaled.reshape(BATCH, N_ROW, strip_pix, C)
    pre_strips = grad_pre.reshape(BATCH, N_ROW, strip_pix, HID)

    def add_grads(index, totals):
        idx = jnp.asarray(index, jnp.int32)
        grad_rows = lax.dynamic_index_in_dim(branch_strips, idx, 1, keepdims=False).reshape(-1, C)
        act_rows = lax.dynamic_index_in_dim(hidden_strips, idx, 1, keepdims=False).reshape(-1, HID)
        norm_rows = lax.dynamic_index_in_dim(scaled_strips, idx, 1, keepdims=False).reshape(-1, C)
        pre_rows = lax.dynamic_index_in_dim(pre_strips, idx, 1, keepdims=False).reshape(-1, HID)
        out_term = lax.dot_general(grad_rows, act_rows, contract_first, preferred_element_type=jnp.float32)
        in_term = lax.dot_general(norm_rows, pre_rows, contract_first, preferred_element_type=jnp.float32)
        return (totals[0] + rounded(out_term), totals[1] + rounded(in_term))
    zero_grads = (jnp.zeros((C, HID), jnp.float32), jnp.zeros((C, HID), jnp.float32))
    out_total, in_total = lax.fori_loop(0, N_ROW, add_grads, zero_grads)
    grad_proj_out = out_total.astype(jnp.bfloat16)
    grad_proj_in = in_total.astype(jnp.bfloat16)

    def add_input(index, total):
        first_col = jnp.asarray(index, jnp.int32) * hid_cols
        pre_block = lax.dynamic_slice_in_dim(grad_pre, first_col, hid_cols, 1)
        weight_block = lax.dynamic_slice_in_dim(proj_in, first_col, hid_cols, 1)
        return total + rounded(lax.dot_general(pre_block, weight_block, contract_last, preferred_element_type=jnp.float32))
    grad_scaled = lax.fori_loop(0, N_COL, add_input, jnp.zeros((pixels, C), jnp.float32))
    weighted = grad_scaled * norm_gain
    mean_one = lax.optimization_barrier(jnp.mean(weighted, axis=1))
    mean_two = lax.optimization_barrier(jnp.mean(weighted * normed, axis=1))
    grad_conv = inv_std[:, None] * (weighted - mean_one[:, None] - normed * mean_two[:, None])
    grad_conv = grad_conv.reshape(BATCH, IMG_H, IMG_W, C)
    grad_pad = jnp.pad(grad_conv, ((0, 0), (reach, reach), (reach, reach), (0, 0)))
    input_grad = taps_sum(grad_pad, dw_kernel, IMG_H, IMG_W, True)
    grad_images = (cotangent.astype(jnp.float32) + input_grad).astype(jnp.bfloat16)
    return (block_out.reshape(BATCH, IMG_H, IMG_W, C), grad_images, grad_proj_in, grad_proj_out)
```

```python
import jax
import jax.numpy as jnp
from jax import lax
from jax.sharding import PartitionSpec as P

C = 2048
KS = 7
F32 = jnp.float32
BF16 = jnp.bfloat16


def taps_sum(padded, dw_kernel, img_rows, img_cols, flipped):
    total = jnp.zeros(padded.shape[:1] + (img_rows, img_cols) + padded.shape[3:], F32)
    reach = 2 * (KS // 2)
    for tap_row in range(KS):
        for tap_col in range(KS):
            off_row = reach - tap_row if flipped else tap_row
            off_col = reach - tap_col if flipped else tap_col
            total = (
                total
                + dw_kernel[tap_row, tap_col]
                * padded[:, off_row : off_row + img_rows, off_col : off_col + img_cols, :]
            )
    return total


def with_halo(block, width):
    count = lax.axis_size("row")
    forward = [(i, i + 1) for i in range(count - 1)]
    backward = [(target, source) for source, target in forward]
    low = lax.ppermute(block[:, -width:], "row", forward)
    high = lax.ppermute(block[:, :width], "row", backward)
    return jnp.concatenate([low, block, high], axis=1)


def gelu_slope(values):
    return (
        0.5 * (1.0 + lax.erf(values * 0.7071067811865476))
        + values * jnp.exp(-0.5 * values * values) * 0.3989422804014327
    )


class Ring:
    def __init__(self):
        count = lax.axis_size("row")
        chips = count // 2
        half = chips // 2
        order = list(range(half)) + list(range(chips - 1, half - 1, -1))
        self.chips = chips
        self.order = jnp.array(order, jnp.int32)
        self.sibling = [(i, i ^ 1) for i in range(count)]
        self.ahead, self.behind = [], []
        for place, chip in enumerate(order):
            after, before = order[(place + 1) % chips], order[(place - 1) % chips]
            self.ahead += [(2 * chip, 2 * after), (2 * chip + 1, 2 * before + 1)]
            self.behind += [(2 * chip, 2 * before), (2 * chip + 1, 2 * after + 1)]
        index = lax.axis_index("row")
        self.core = index % 2
        places = [order.index(chip) for chip in range(chips)]
        self.place = jnp.array(places, jnp.int32)[index // 2]
        self.sense = 1 - 2 * self.core
        self.groups = [list(range(0, count, 2)), list(range(1, count, 2))]

    def chip_at(self, steps):
        return self.order[(self.place + self.sense * steps + self.chips) % self.chips]

    def swap(self, block):
        return lax.ppermute(block, "row", self.sibling)

    def gather(self, block):
        half = self.chips // 2
        panel = jnp.zeros((self.chips,) + block.shape, block.dtype)
        panel = lax.dynamic_update_index_in_dim(panel, block, self.chip_at(0), 0)
        one, two = block, block
        for step in range(1, half + 1):
            one = lax.ppermute(one, "row", self.ahead)
            panel = lax.dynamic_update_index_in_dim(panel, one, self.chip_at(-step), 0)
            if step < half:
                two = lax.ppermute(two, "row", self.behind)
                panel = lax.dynamic_update_index_in_dim(panel, two, self.chip_at(step), 0)
        return panel.reshape(-1, block.shape[-1])

    def scatter(self, whole):
        half = self.chips // 2
        parts = whole.reshape(self.chips, -1, whole.shape[-1])

        def part(steps):
            return lax.dynamic_index_in_dim(parts, self.chip_at(steps), 0, False).astype(F32)

        one = part(-half)
        two = part(half - 1)
        for step in range(half - 1, 0, -1):
            one = lax.ppermute(one.astype(BF16), "row", self.behind).astype(F32) + part(-step)
            if step < half - 1:
                two = lax.ppermute(two.astype(BF16), "row", self.ahead).astype(F32) + part(step)
        one = lax.ppermute(one.astype(BF16), "row", self.behind).astype(F32)
        if half > 1:
            two = lax.ppermute(two.astype(BF16), "row", self.ahead).astype(F32)
        else:
            two = 0.0
        return one + two + part(0)


def chip_block(ring, weight):
    width = weight.shape[1] // 2
    keep = lax.dynamic_slice_in_dim(weight, ring.core * width, width, 1)
    give = lax.dynamic_slice_in_dim(weight, (1 - ring.core) * width, width, 1)
    other = ring.swap(give)
    return jnp.where(
        ring.core == 0,
        jnp.concatenate([keep, other], axis=0),
        jnp.concatenate([other, keep], axis=0),
    )


def own_rows(ring, block):
    rows = block.shape[0] // 2
    keep = lax.dynamic_slice_in_dim(block, ring.core * rows, rows, 0)
    give = lax.dynamic_slice_in_dim(block, (1 - ring.core) * rows, rows, 0)
    other = ring.swap(give)
    return jnp.where(
        ring.core == 0,
        jnp.concatenate([keep, other], axis=1),
        jnp.concatenate([other, keep], axis=1),
    )


UP = [(0, 1), (1, 2), (2, 3)]
DOWN = [(1, 0), (2, 1), (3, 2)]
ACROSS = [(0, 2), (1, 3), (2, 0), (3, 1)]


def col_gather(block):
    count = lax.axis_size("col")
    if count != 4:
        return lax.all_gather(block, "col", axis=1, tiled=True)
    z = lax.axis_index("col")
    across = lax.ppermute(block, "col", ACROSS)
    below = lax.ppermute(block, "col", UP)
    above = lax.ppermute(block, "col", DOWN)
    far = lax.ppermute(across, "col", [(1, 0), (2, 3)])
    below = jnp.where(z == 0, far, below)
    above = jnp.where(z == 3, far, above)
    width = block.shape[1]
    full = jnp.zeros((block.shape[0], width * count), block.dtype)
    for shift, part in ((0, block), (1, above), (2, across), (3, below)):
        full = lax.dynamic_update_slice_in_dim(full, part, (z + shift) % count * width, 1)
    return full


def col_scatter(whole):
    count = lax.axis_size("col")
    if count != 4:
        return lax.psum_scatter(whole, "col", scatter_dimension=1, tiled=True).astype(F32)
    z = lax.axis_index("col")
    width = whole.shape[1] // count

    def part(index):
        return lax.dynamic_slice_in_dim(whole, index * width, width, 1)

    far = lax.ppermute(part(3 - z), "col", [(0, 1), (3, 2)])
    below = lax.ppermute(part(jnp.minimum(z + 1, 3)), "col", UP)
    above = lax.ppermute(part(jnp.maximum(z - 1, 0)), "col", DOWN)
    pair = (part((z + 2) % count).astype(F32) + far.astype(F32)).astype(BF16)
    across = lax.ppermute(pair, "col", ACROSS)
    return part(z).astype(F32) + below.astype(F32) + above.astype(F32) + across.astype(F32)


def col_all(small):
    count = lax.axis_size("col")
    shifts = [
        lax.ppermute(small, "col", [(i, (i + step) % count) for i in range(count)])
        for step in range(1, count)
    ]
    return jnp.stack([small] + shifts)


def on_device(images, dw_kernel, norm_gain, proj_in, proj_out, layer_scale, cotangent):
    img_batch, strip_rows, img_cols, local_ch = images.shape
    pixels = img_batch * strip_rows * img_cols
    reach = KS // 2
    contract_last = (((1,), (1,)), ((), ()))
    contract_first = (((0,), (0,)), ((), ()))
    ring = Ring()

    in_panel = ring.gather(chip_block(ring, proj_in))
    out_panel = lax.all_gather(
        chip_block(ring, proj_out), "row", axis=0, tiled=True, axis_index_groups=ring.groups
    )
    cot_flat = cotangent.reshape(pixels, local_ch).astype(F32)
    grad_branch = (cot_flat * layer_scale).astype(BF16)
    strip_grad = col_gather(grad_branch)
    full_grad = jnp.concatenate([strip_grad, ring.swap(strip_grad)], axis=0)

    rimmed = with_halo(images, reach)
    padded = jnp.pad(rimmed.astype(F32), ((0, 0), (0, 0), (reach, reach), (0, 0)))
    conv_out = taps_sum(padded, dw_kernel, strip_rows, img_cols, False).reshape(pixels, local_ch)
    own_mean = jnp.mean(conv_out, axis=1)
    own_dev = conv_out - own_mean[:, None]
    stats = col_all(jnp.stack([own_mean, jnp.sum(own_dev * own_dev, axis=1)]))
    row_mean = jnp.mean(stats[:, 0], axis=0)
    spread = stats[:, 0] - row_mean
    row_var = jnp.sum(stats[:, 1] + local_ch * (spread * spread), axis=0) / C
    inv_std = lax.rsqrt(row_var + 1e-06)
    normed = (conv_out - row_mean[:, None]) * inv_std[:, None]
    scaled = (normed * norm_gain).astype(BF16)
    strip_in = col_gather(scaled)
    full_in = jnp.concatenate([strip_in, ring.swap(strip_in)], axis=0)

    hidden_pre = jnp.dot(full_in, in_panel, preferred_element_type=F32)
    hidden = jax.nn.gelu(hidden_pre, approximate=False).astype(BF16)
    out_part = lax.dot_general(
        full_grad, hidden, contract_first, preferred_element_type=F32
    ).astype(BF16)
    out_rows = lax.psum_scatter(
        out_part, "row", scatter_dimension=0, tiled=True, axis_index_groups=ring.groups
    )
    grad_hidden = jnp.dot(full_grad, out_panel, preferred_element_type=F32)
    grad_pre = (grad_hidden * gelu_slope(hidden_pre)).astype(BF16)

    def strip_sum(both):
        both = both.astype(BF16)
        other = ring.swap(both[pixels:])
        return (both[:pixels].astype(F32) + other.astype(F32)).astype(BF16)

    back_part = lax.dot_general(grad_pre, in_panel, contract_last, preferred_element_type=F32)
    grad_scaled = col_scatter(strip_sum(back_part))
    in_part = lax.dot_general(
        full_in, grad_pre, contract_first, preferred_element_type=F32
    ).astype(BF16)
    in_rows = ring.scatter(in_part)
    contrib = lax.dot_general(hidden, out_panel, contract_last, preferred_element_type=F32)
    branch = col_scatter(strip_sum(contrib))
    residual_in = images.reshape(pixels, local_ch).astype(F32)
    block_out = (residual_in + layer_scale * branch).astype(BF16).reshape(images.shape)

    weighted = grad_scaled * norm_gain
    sums = jnp.sum(
        col_all(jnp.stack([jnp.sum(weighted, axis=1), jnp.sum(weighted * normed, axis=1)])), axis=0
    )
    grad_conv = inv_std[:, None] * (
        weighted - sums[0][:, None] / C - normed * sums[1][:, None] / C
    )
    grad_conv = grad_conv.reshape(images.shape)
    grad_rim = with_halo(grad_conv.astype(BF16), reach).astype(F32)
    grad_pad = jnp.pad(grad_rim, ((0, 0), (0, 0), (reach, reach), (0, 0)))
    input_grad = taps_sum(grad_pad, dw_kernel, strip_rows, img_cols, True)
    grad_images = (cotangent.astype(F32) + input_grad).astype(BF16)
    return (
        block_out,
        grad_images,
        own_rows(ring, in_rows.astype(BF16)),
        own_rows(ring, out_rows),
    )


def solution(mesh):
    placed = (
        P(None, "row", None, "col"),
        P(None, None, "col"),
        P("col"),
        P("row", "col"),
        P("row", "col"),
        P("col"),
        P(None, "row", None, "col"),
    )
    return jax.shard_map(
        on_device,
        mesh=mesh,
        in_specs=placed,
        out_specs=(
            P(None, "row", None, "col"),
            P(None, "row", None, "col"),
            P("row", "col"),
            P("row", "col"),
        ),
        check_vma=False,
    )
```

```python
import functools

import jax
import jax.numpy as jnp
from jax import lax
from jax.experimental import pallas as pl
from jax.experimental.pallas import tpu as pltpu
from jax.sharding import PartitionSpec as P

C = 2048
KS = 7
REACH = KS // 2
F32 = jnp.float32
BF16 = jnp.bfloat16
LAST = (((1,), (1,)), ((), ()))
FIRST = (((0,), (0,)), ((), ()))
SIBLING = [(i, i ^ 1) for i in range(8)]
CHIPS = (0, 1, 3, 2)
UP = [(0, 1), (1, 2), (2, 3)]
DOWN = [(1, 0), (2, 1), (3, 2)]
ACROSS = [(0, 2), (1, 3), (2, 0), (3, 1)]
SAME_CORE = [[0, 2, 4, 6], [1, 3, 5, 7]]
ANY = pl.BlockSpec(memory_space=pl.ANY)
VMEM = pl.BlockSpec(memory_space=pltpu.VMEM)
PARAMS = pltpu.CompilerParams(vmem_limit_bytes=52 * 2**20)
HINT = pl.CostEstimate(flops=0, bytes_accessed=0, transcendentals=0)


def ring_pairs(sense):
    pairs = []
    for place, chip in enumerate(CHIPS):
        for core in (0, 1):
            step = sense if core == 0 else -sense
            pairs.append((2 * chip + core, 2 * CHIPS[(place + step) % 4] + core))
    return pairs


AHEAD = ring_pairs(1)
BEHIND = ring_pairs(-1)


def shape(dims, dtype=BF16):
    return jax.ShapeDtypeStruct(dims, dtype)


def call(body, ids, arrays, grid, ins, outs, shapes, scratch=(), after=(), aliases=None):
    count = len(arrays)

    def kernel(ids_ref, *refs):
        body(ids_ref, *refs[:count], *refs[count + len(after) :])

    return pl.pallas_call(
        kernel,
        grid_spec=pltpu.PrefetchScalarGridSpec(
            num_scalar_prefetch=1,
            grid=grid,
            in_specs=list(ins) + [ANY] * len(after),
            out_specs=outs,
            scratch_shapes=scratch,
        ),
        out_shape=shapes,
        compiler_params=PARAMS,
        cost_estimate=HINT,
        input_output_aliases=aliases or {},
    )(ids, *arrays, *after)


def later(ids, array, after):
    return call(
        lambda *refs: None, ids, [array], (), [ANY], ANY, shape(array.shape, array.dtype),
        after=after, aliases={1: 0},
    )


def whole(dims):
    return pl.BlockSpec(dims, lambda *_: (0,) * len(dims))


def make_ids():
    z = lax.axis_index("col")
    row = lax.axis_index("row")
    core = row % 2
    sense = 1 - 2 * core
    places = jnp.array([CHIPS.index(chip) for chip in range(4)], jnp.int32)
    order = jnp.array(CHIPS, jnp.int32)
    place = places[row // 2]
    ring = [order[(place + sense * step + 4) % 4] for step in (0, -1, 1, 2)]
    return jnp.stack([z, (z + 1) % 4, (z + 2) % 4, (z + 3) % 4, core] + ring).astype(jnp.int32)


def move(body, ids, arrays, shapes, count, after=()):
    def kernel(ids_ref, *refs):
        sems = refs[-1]
        pairs = list(body(ids_ref, refs[: len(arrays)], refs[len(arrays) : -1]))
        copies = [pltpu.make_async_copy(src, dst, sems.at[i]) for i, (_, src, dst) in enumerate(pairs)]
        for (when, _, _), copy in zip(pairs, copies):
            if when is None:
                copy.start()
            else:
                pl.when(when)(copy.start)
        for (when, _, _), copy in zip(pairs, copies):
            if when is None:
                copy.wait()
            else:
                pl.when(when)(copy.wait)

    return call(
        kernel, ids, arrays, (), [ANY] * len(arrays), [VMEM] * len(shapes), shapes,
        [pltpu.SemaphoreType.DMA((count,))], after,
    )


def start_of(index, size):
    return pl.ds(pl.multiple_of(index * size, size), size)


def give_half(ids, weight):
    rows, cols = weight.shape

    def body(i, s, t):
        yield None, s[0].at[:, start_of(1 - i[4], cols // 2)], t[0]

    return move(body, ids, [weight], [shape((rows, cols // 2))], 1)[0]


def chip_rows(ids, weight, other):
    rows, cols = weight.shape

    def body(i, s, t):
        yield None, s[0].at[:, start_of(i[4], cols // 2)], t[0].at[start_of(i[4], rows)]
        yield None, s[1], t[0].at[start_of(1 - i[4], rows)]

    return move(body, ids, [weight, other], [shape((2 * rows, cols // 2))], 2)[0]


def stack_chips(ids, blocks):
    rows, cols = blocks[0].shape

    def body(i, s, t):
        for k in range(4):
            yield None, s[k], t[0].at[start_of(i[5 + k], rows)]

    return move(body, ids, blocks, [shape((4 * rows, cols))], 4)[0]


def ring_gather(ids, block):
    one = lax.ppermute(block, "row", AHEAD)
    two = lax.ppermute(block, "row", BEHIND)
    far = lax.ppermute(one, "row", AHEAD)
    return stack_chips(ids, [block, one, two, far])


def col_gather(ids, block, before_far=(), before_end=()):
    rows, cols = block.shape
    across = lax.ppermute(block, "col", ACROSS)
    above = lax.ppermute(block, "col", DOWN)
    below = lax.ppermute(block, "col", UP)
    if before_far:
        across = later(ids, across, before_far)
    far = lax.ppermute(across, "col", [(1, 0), (2, 3)])

    def body(i, s, t):
        def to(k):
            return t[0].at[:, start_of(i[k], cols)]

        z = i[0]
        yield None, s[0], to(0)
        yield None, s[2], to(2)
        yield z < 3, s[1], to(1)
        yield z == 3, s[4], to(1)
        yield z > 0, s[3], to(3)
        yield z == 0, s[4], to(3)

    return move(
        body, ids, [block, above, across, below, far], [shape((rows, 4 * cols))], 6, before_end
    )[0]


def gelu_parts(v):
    cdf = 0.5 * (1.0 + lax.erf(v * 0.7071067811865476))
    return v * cdf, cdf + v * jnp.exp(-0.5 * v * v) * 0.3989422804014327


TILE = 256


def expand(ids, own, sib, panel):
    rows = own.shape[0]
    hid = panel.shape[1]

    def kernel(ids_ref, own_ref, sib_ref, w_ref, hidden_ref, slope_ref):
        for half, x in enumerate((own_ref, sib_ref)):
            at = pl.ds(half * rows, rows)
            pre = jnp.dot(x[...], w_ref[...], preferred_element_type=F32)
            act, slope = gelu_parts(pre)
            hidden_ref[at] = act.astype(BF16)
            slope_ref[at] = slope.astype(BF16)

    tile = pl.BlockSpec((2 * rows, TILE), lambda t, i: (0, t))
    return call(
        kernel, ids, [own, sib, panel], (hid // TILE,),
        [whole(own.shape), whole(sib.shape), pl.BlockSpec((C, TILE), lambda t, i: (0, t))],
        [tile, tile], [shape((2 * rows, hid))] * 2,
    )


def expand_grad(ids, own, sib, panel, slope, after):
    rows = own.shape[0]
    hid = slope.shape[1]
    steps = hid // TILE

    def kernel(ids_ref, own_ref, sib_ref, w_ref, slope_ref, out_ref):
        for half, x in enumerate((own_ref, sib_ref)):
            at = pl.ds(half * rows, rows)
            back = jnp.dot(x[...], w_ref[...], preferred_element_type=F32)
            out_ref[at] = (back * slope_ref[at].astype(F32)).astype(BF16)

    tile = pl.BlockSpec((2 * rows, TILE), lambda t, i: (0, t))
    return call(
        kernel, ids, [own, sib, panel, slope], (steps,),
        [
            whole(own.shape),
            whole(sib.shape),
            pl.BlockSpec((C, TILE), lambda t, i: (0, i[4] * steps + t)),
            tile,
        ],
        tile, shape((2 * rows, hid)), after=after,
    )


def weight_grad(ids, own, sib, right, slots, after=()):
    rows = own.shape[0]
    hid = right.shape[1]
    steps = 512 // TILE

    def kernel(ids_ref, own_ref, sib_ref, r_ref, *outs):
        acc = lax.dot_general(own_ref[...], r_ref[:rows], FIRST, preferred_element_type=F32)
        acc += lax.dot_general(sib_ref[...], r_ref[rows:], FIRST, preferred_element_type=F32)
        if not slots:
            outs[0][...] = acc.astype(BF16)
            return
        for k in range(4):
            @pl.when(pl.program_id(0) == k)
            def _():
                outs[k][...] = acc.astype(BF16)

    if slots:
        order = (8, 7, 6, 5)

        def column(s, t, i):
            first = jnp.where(s == 0, i[8], jnp.where(s == 1, i[7], jnp.where(s == 2, i[6], i[5])))
            return 0, first * steps + t

        outs = [
            pl.BlockSpec(
                (TILE, hid),
                lambda s, t, i, k=k: (jnp.where(s == k, t, jnp.where(s < k, 0, steps - 1)), 0),
            )
            for k in range(4)
        ]
        shapes = [shape((512, hid))] * 4
    else:
        def column(s, t, i):
            return 0, s * steps + t

        outs = pl.BlockSpec((TILE, hid), lambda s, t, i: (s * steps + t, 0))
        shapes = shape((C, hid))
    cut = pl.BlockSpec((rows, TILE), column)
    return call(
        kernel, ids, [own, sib, right], (4, steps), [cut, cut, whole(right.shape)], outs, shapes,
        after=after,
    )


def contract_sib(ids, left, panel, offset, after=()):
    rows = left.shape[0] // 2
    hid = left.shape[1]

    def kernel(ids_ref, x_ref, w_ref, out_ref):
        out_ref[...] = lax.dot_general(
            x_ref[...], w_ref[...], LAST, preferred_element_type=F32
        ).astype(BF16)

    return call(
        kernel, ids, [left, panel], (C // 512,),
        [
            pl.BlockSpec((rows, hid), lambda t, i: (1, 0)),
            pl.BlockSpec((512, hid), lambda t, i: (t, i[4] * offset)),
        ],
        pl.BlockSpec((rows, 512), lambda t, i: (0, t)), shape((rows, C)), after=after,
    )


def contract_own(ids, left, panel, other, offset, after=()):
    rows = left.shape[0] // 2
    hid = left.shape[1]

    def kernel(ids_ref, x_ref, w_ref, o_ref, *outs):
        acc = lax.dot_general(x_ref[...], w_ref[...], LAST, preferred_element_type=F32)
        acc = (acc + o_ref[...].astype(F32)).astype(BF16)
        step = pl.program_id(0)
        for k in range(4):
            @pl.when(step == k)
            def _():
                outs[k][...] = acc

        @pl.when(step == jnp.where(ids_ref[0] == 0, 3, 1))
        def _():
            outs[4][...] = acc

    def pick(t, i):
        return jnp.where(t == 0, i[0], jnp.where(t == 1, i[1], jnp.where(t == 2, i[2], i[3])))

    return call(
        kernel, ids, [left, panel, other], (4,),
        [
            pl.BlockSpec((rows, hid), lambda t, i: (0, 0)),
            pl.BlockSpec((512, hid), lambda t, i: (pick(t, i), i[4] * offset)),
            pl.BlockSpec((rows, 512), lambda t, i: (0, pick(t, i))),
        ],
        [whole((rows, 512))] * 5, [shape((rows, 512))] * 5, after=after,
    )


def col_scatter(blocks):
    own, after, across, before, far = blocks
    far = lax.ppermute(far, "col", [(0, 1), (3, 2)])
    below = lax.ppermute(after, "col", UP)
    above = lax.ppermute(before, "col", DOWN)
    pair = (across.astype(F32) + far.astype(F32)).astype(BF16)
    across = lax.ppermute(pair, "col", ACROSS)
    return own.astype(F32) + below.astype(F32) + above.astype(F32) + across.astype(F32)


def ring_scatter(blocks):
    far, ahead, behind, own = blocks
    one = lax.ppermute(far, "row", BEHIND)
    two = lax.ppermute(ahead, "row", AHEAD)
    one = lax.ppermute((one.astype(F32) + behind.astype(F32)).astype(BF16), "row", BEHIND)
    return (own.astype(F32) + one.astype(F32) + two.astype(F32)).astype(BF16)


def give_rows(ids, block):
    rows, cols = block.shape

    def body(i, s, t):
        yield None, s[0].at[start_of(1 - i[4], rows // 2)], t[0]

    return move(body, ids, [block], [shape((rows // 2, cols))], 1)[0]


def own_rows(ids, block):
    rows, cols = block.shape
    other = lax.ppermute(give_rows(ids, block), "row", SIBLING)

    def body(i, s, t):
        yield None, s[0].at[start_of(i[4], rows // 2)], t[0].at[:, start_of(i[4], cols)]
        yield None, s[1], t[0].at[:, start_of(1 - i[4], cols)]

    return move(body, ids, [block, other], [shape((rows // 2, 2 * cols))], 2)[0]


def taps(ids, low, mid, high, dw_kernel, flipped, extra=None, after=()):
    images, rows, width, chans = mid.shape
    lanes = 128
    edge = 8

    def kernel(ids_ref, *refs):
        low_ref, mid_ref, high_ref, dw_ref = refs[:4]
        out_ref, pad_ref = refs[-2:]
        pad_ref[:, :edge] = jnp.zeros((rows + 2 * REACH, edge, lanes), F32)
        pad_ref[:, edge + width :] = jnp.zeros((rows + 2 * REACH, edge, lanes), F32)
        pad_ref[:REACH, edge : edge + width] = low_ref[0].astype(F32)
        pad_ref[REACH : REACH + rows, edge : edge + width] = mid_ref[0].astype(F32)
        pad_ref[REACH + rows :, edge : edge + width] = high_ref[0].astype(F32)
        totals = [jnp.zeros((width, lanes), F32)] * rows
        for off_col in range(KS):
            tap_col = KS - 1 - off_col if flipped else off_col
            for place in range(rows + 2 * REACH):
                line = pad_ref[place, pl.ds(edge - REACH + off_col, width)]
                for row in range(rows):
                    off_row = place - row
                    if 0 <= off_row < KS:
                        tap_row = KS - 1 - off_row if flipped else off_row
                        totals[row] += dw_ref[pl.ds(tap_row * KS + tap_col, 1)] * line
        for row in range(rows):
            if extra is None:
                out_ref[0, row] = totals[row]
            else:
                out_ref[0, row] = (refs[4][0, row].astype(F32) + totals[row]).astype(BF16)

    def strip(count):
        return pl.BlockSpec((1, count, width, lanes), lambda b, c, i: (b, 0, 0, c))

    arrays = [low, mid, high, dw_kernel.reshape(KS * KS, chans)]
    ins = [strip(REACH), strip(rows), strip(REACH), pl.BlockSpec((KS * KS, lanes), lambda b, c, i: (0, c))]
    if extra is not None:
        arrays.append(extra)
        ins.append(strip(rows))
    return call(
        kernel, ids, arrays, (images, chans // lanes), ins, strip(rows),
        shape(mid.shape, F32 if extra is None else BF16),
        [pltpu.VMEM((rows + 2 * REACH, width + 2 * edge, lanes), F32)], after,
    )


def rims(block):
    count = lax.axis_size("row")
    forward = [(i, i + 1) for i in range(count - 1)]
    backward = [(i + 1, i) for i in range(count - 1)]
    low = lax.ppermute(block[:, -REACH:], "row", forward)
    high = lax.ppermute(block[:, :REACH], "row", backward)
    return low, high


def col_all(small):
    count = lax.axis_size("col")
    shifts = [
        lax.ppermute(small, "col", [(i, (i + step) % count) for i in range(count)])
        for step in range(1, count)
    ]
    return jnp.stack([small] + shifts)


def on_device(images, dw_kernel, norm_gain, proj_in, proj_out, layer_scale, cotangent):
    local_ch = images.shape[3]
    pixels = images.shape[0] * images.shape[1] * images.shape[2]
    ids = make_ids()

    def swap(block):
        return lax.ppermute(block, "row", SIBLING)

    out_panel = lax.all_gather(proj_out, "row", axis=0, tiled=True)
    cot_flat = cotangent.reshape(pixels, local_ch).astype(F32)
    grad_branch = (cot_flat * layer_scale).astype(BF16)
    low, high = rims(images)
    in_block = chip_rows(ids, proj_in, swap(give_half(ids, proj_in)))
    in_panel = ring_gather(ids, in_block)
    grad_own = col_gather(ids, grad_branch, before_end=[in_panel])
    grad_sib = swap(grad_own)

    conv_out = taps(ids, low, images, high, dw_kernel, False, after=[in_block]).reshape(pixels, local_ch)
    own_mean = jnp.mean(conv_out, axis=1)
    own_dev = conv_out - own_mean[:, None]
    stats = col_all(jnp.stack([own_mean, jnp.sum(own_dev * own_dev, axis=1)]))
    row_mean = jnp.mean(stats[:, 0], axis=0)
    spread = stats[:, 0] - row_mean
    row_var = jnp.sum(stats[:, 1] + local_ch * (spread * spread), axis=0) / C
    inv_std = lax.rsqrt(row_var + 1e-06)
    normed = (conv_out - row_mean[:, None]) * inv_std[:, None]
    scaled = (normed * norm_gain).astype(BF16)
    in_own = col_gather(ids, scaled, before_far=[grad_own])
    in_sib = swap(in_own)

    hidden, slope = expand(ids, in_own, in_sib, in_panel)
    out_part = weight_grad(ids, grad_own, grad_sib, hidden, False)
    out_rows = lax.psum_scatter(
        out_part, "row", scatter_dimension=0, tiled=True, axis_index_groups=SAME_CORE
    )
    grad_pre = expand_grad(ids, grad_own, grad_sib, out_panel, slope, [out_part])
    back_give = contract_sib(ids, grad_pre, in_panel, 0)
    back_sib = swap(back_give)
    in_parts = weight_grad(ids, in_own, in_sib, grad_pre, True, [back_give])
    back = contract_own(ids, grad_pre, in_panel, back_sib, 0, [in_parts[0]])
    grad_scaled = col_scatter(back)
    in_rows = ring_scatter(in_parts)
    branch_give = contract_sib(ids, hidden, out_panel, 1, [back[0]])
    branch = col_scatter(contract_own(ids, hidden, out_panel, swap(branch_give), 1))
    residual_in = images.reshape(pixels, local_ch).astype(F32)
    block_out = (residual_in + layer_scale * branch).astype(BF16).reshape(images.shape)

    weighted = grad_scaled * norm_gain
    sums = jnp.sum(
        col_all(jnp.stack([jnp.sum(weighted, axis=1), jnp.sum(weighted * normed, axis=1)])), axis=0
    )
    grad_conv = inv_std[:, None] * (
        weighted - sums[0][:, None] / C - normed * sums[1][:, None] / C
    )
    grad_conv = grad_conv.astype(BF16).reshape(images.shape)
    low, high = rims(grad_conv)
    grad_images = taps(ids, low, grad_conv, high, dw_kernel, True, cotangent)
    return block_out, grad_images, own_rows(ids, in_rows), own_rows(ids, out_rows)


def with_halo(block, sides, width):
    for axis, dim in sides:
        count = lax.axis_size(axis)
        forward = [(i, i + 1) for i in range(count - 1)]
        backward = [(target, source) for source, target in forward]
        low = lax.ppermute(
            lax.slice_in_dim(block, block.shape[dim] - width, None, axis=dim), axis, forward
        )
        high = lax.ppermute(lax.slice_in_dim(block, 0, width, axis=dim), axis, backward)
        block = jnp.concatenate([low, block, high], axis=dim)
    return block


def taps_sum(padded, dw_kernel, img_rows, img_cols, flipped):
    total = jnp.zeros(padded.shape[:1] + (img_rows, img_cols) + padded.shape[3:], jnp.float32)
    reach = 2 * (KS // 2)
    for tap_row in range(KS):
        for tap_col in range(KS):
            off_row = reach - tap_row if flipped else tap_row
            off_col = reach - tap_col if flipped else tap_col
            total = (
                total
                + dw_kernel[tap_row, tap_col]
                * padded[:, off_row : off_row + img_rows, off_col : off_col + img_cols, :]
            )
    return total


def gelu_slope(values):
    return (
        0.5 * (1.0 + lax.erf(values * 0.7071067811865476))
        + values * jnp.exp(-0.5 * values * values) * 0.3989422804014327
    )


def on_any_mesh(images, dw_kernel, norm_gain, proj_in, proj_out, layer_scale, cotangent):
    img_batch, strip_rows, img_cols, local_ch = images.shape
    pixels = img_batch * strip_rows * img_cols
    reach = KS // 2
    contract_last = (((1,), (1,)), ((), ()))
    contract_first = (((0,), (0,)), ((), ()))
    rimmed = with_halo(images, (("row", 1),), reach)
    padded = jnp.pad(rimmed.astype(jnp.float32), ((0, 0), (0, 0), (reach, reach), (0, 0)))
    conv_out = taps_sum(padded, dw_kernel, strip_rows, img_cols, False).reshape(pixels, local_ch)
    row_mean = lax.psum(jnp.sum(conv_out, axis=1), "col") / C
    centred = conv_out - row_mean[:, None]
    row_var = lax.psum(jnp.sum(centred * centred, axis=1), "col") / C
    inv_std = lax.rsqrt(row_var + 1e-06)
    normed = centred * inv_std[:, None]
    scaled = (normed * norm_gain).astype(jnp.bfloat16)
    full_in = lax.all_gather(scaled, "col", axis=1, tiled=True)
    in_panel = lax.all_gather(proj_in, "row", axis=0, tiled=True)
    out_panel = lax.all_gather(proj_out, "row", axis=0, tiled=True)
    hidden_pre = jnp.dot(full_in, in_panel, preferred_element_type=jnp.float32)
    hidden = jax.nn.gelu(hidden_pre, approximate=False).astype(jnp.bfloat16)
    contrib = lax.dot_general(hidden, out_panel, contract_last, preferred_element_type=jnp.float32)
    branch = lax.psum_scatter(
        contrib.astype(jnp.bfloat16), "col", scatter_dimension=1, tiled=True
    ).astype(jnp.float32)
    residual_in = images.reshape(pixels, local_ch).astype(jnp.float32)
    block_out = (residual_in + layer_scale * branch).astype(jnp.bfloat16).reshape(images.shape)
    cot_flat = cotangent.reshape(pixels, local_ch).astype(jnp.float32)
    grad_branch = (cot_flat * layer_scale).astype(jnp.bfloat16)
    full_grad = lax.all_gather(grad_branch, "col", axis=1, tiled=True)
    grad_proj_out = lax.psum_scatter(
        lax.dot_general(
            full_grad, hidden, contract_first, preferred_element_type=jnp.float32
        ).astype(jnp.bfloat16),
        "row",
        scatter_dimension=0,
        tiled=True,
    )
    grad_hidden = jnp.dot(full_grad, out_panel, preferred_element_type=jnp.float32)
    grad_pre = (grad_hidden * gelu_slope(hidden_pre)).astype(jnp.bfloat16)
    grad_proj_in = lax.psum_scatter(
        lax.dot_general(
            full_in, grad_pre, contract_first, preferred_element_type=jnp.float32
        ).astype(jnp.bfloat16),
        "row",
        scatter_dimension=0,
        tiled=True,
    )
    back_part = lax.dot_general(
        grad_pre, in_panel, contract_last, preferred_element_type=jnp.float32
    )
    grad_scaled = lax.psum_scatter(
        back_part.astype(jnp.bfloat16), "col", scatter_dimension=1, tiled=True
    ).astype(jnp.float32)
    weighted = grad_scaled * norm_gain
    sum_one, sum_two = lax.psum(
        (jnp.sum(weighted, axis=1), jnp.sum(weighted * normed, axis=1)), "col"
    )
    grad_conv = inv_std[:, None] * (weighted - sum_one[:, None] / C - normed * sum_two[:, None] / C)
    grad_conv = grad_conv.reshape(img_batch, strip_rows, img_cols, local_ch)
    grad_rim = with_halo(grad_conv.astype(jnp.bfloat16), (("row", 1),), reach).astype(
        grad_conv.dtype
    )
    grad_pad = jnp.pad(grad_rim, ((0, 0), (0, 0), (reach, reach), (0, 0)))
    input_grad = taps_sum(grad_pad, dw_kernel, strip_rows, img_cols, True)
    grad_images = (cotangent.astype(jnp.float32) + input_grad).astype(jnp.bfloat16)
    return (block_out, grad_images, grad_proj_in, grad_proj_out)


def solution(mesh):
    tuned = mesh.shape["row"] == 8 and mesh.shape["col"] == 4
    placed = (
        P(None, "row", None, "col"),
        P(None, None, "col"),
        P("col"),
        P("row", "col"),
        P("row", "col"),
        P("col"),
        P(None, "row", None, "col"),
    )
    return jax.shard_map(
        on_device if tuned else on_any_mesh,
        mesh=mesh,
        in_specs=placed,
        out_specs=(
            P(None, "row", None, "col"),
            P(None, "row", None, "col"),
            P("row", "col"),
            P("row", "col"),
        ),
        check_vma=False,
    )
```

```python
import functools

import jax
import jax.numpy as jnp
import numpy as np
from jax import lax
from jax.experimental import pallas as pl
from jax.experimental.pallas import tpu as pltpu
from jax.sharding import PartitionSpec as P

C = 2048
KS = 7
REACH = KS // 2
F32 = jnp.float32
BF16 = jnp.bfloat16
LAST = (((1,), (1,)), ((), ()))
FIRST = (((0,), (0,)), ((), ()))
SIBLING = [(i, i ^ 1) for i in range(8)]
UP = [(0, 1), (1, 2), (2, 3)]
DOWN = [(1, 0), (2, 1), (3, 2)]
ACROSS = [(0, 2), (1, 3), (2, 0), (3, 1)]
SAME_CORE = [[0, 2, 4, 6], [1, 3, 5, 7]]
ANY = pl.BlockSpec(memory_space=pl.ANY)
VMEM = pl.BlockSpec(memory_space=pltpu.VMEM)
PARAMS = pltpu.CompilerParams(vmem_limit_bytes=52 * 2**20)
HINT = pl.CostEstimate(flops=0, bytes_accessed=0, transcendentals=0)
WORK = pl.CostEstimate(flops=2**32, bytes_accessed=12 * 2**20, transcendentals=0)


def shape(dims, dtype=BF16):
    return jax.ShapeDtypeStruct(dims, dtype)


def call(
    body, ids, arrays, grid, ins, outs, shapes, scratch=(), after=(), aliases=None
):
    count = len(arrays)

    def kernel(ids_ref, *refs):
        body(ids_ref, *refs[:count], *refs[count + len(after) :])

    return pl.pallas_call(
        kernel,
        grid_spec=pltpu.PrefetchScalarGridSpec(
            num_scalar_prefetch=1,
            grid=grid,
            in_specs=list(ins) + [ANY] * len(after),
            out_specs=outs,
            scratch_shapes=scratch,
        ),
        out_shape=shapes,
        compiler_params=PARAMS,
        cost_estimate=WORK if grid else HINT,
        input_output_aliases=aliases or {},
    )(ids, *arrays, *after)


def later(ids, array, after):
    return call(
        lambda *refs: None, ids, [array], (), [ANY], ANY, shape(array.shape, array.dtype),
        after=after, aliases={1: 0},
    )


def whole(dims):
    return pl.BlockSpec(dims, lambda *_: (0,) * len(dims))


def make_ids():
    table = np.zeros((8, 4, 5), np.int32)
    for row in range(8):
        for z in range(4):
            table[row, z] = [z, (z + 1) % 4, (z + 2) % 4, (z + 3) % 4, row % 2]
    place = (lax.axis_index("row"), lax.axis_index("col"), 0)
    return lax.dynamic_slice(jnp.asarray(table), place, (1, 1, 5)).reshape(5)


def move(body, ids, arrays, shapes, count, after=()):
    def kernel(ids_ref, *refs):
        sems = refs[-1]
        pairs = list(body(ids_ref, refs[: len(arrays)], refs[len(arrays) : -1]))
        copies = [pltpu.make_async_copy(src, dst, sems.at[i]) for i, (_, src, dst) in enumerate(pairs)]
        for (when, _, _), copy in zip(pairs, copies):
            if when is None:
                copy.start()
            else:
                pl.when(when)(copy.start)
        for (when, _, _), copy in zip(pairs, copies):
            if when is None:
                copy.wait()
            else:
                pl.when(when)(copy.wait)

    return call(
        kernel, ids, arrays, (), [ANY] * len(arrays), [VMEM] * len(shapes), shapes,
        [pltpu.SemaphoreType.DMA((count,))], after,
    )


def start_of(index, size):
    return pl.ds(pl.multiple_of(index * size, size), size)


def col_send(block):
    across = lax.ppermute(block, "col", ACROSS)
    above = lax.ppermute(block, "col", DOWN)
    below = lax.ppermute(block, "col", UP)
    return block, above, across, below


def col_gather(ids, parts, before_far):
    block, above, across, below = parts
    rows, cols = block.shape
    across = later(ids, across, before_far)
    far = lax.ppermute(across, "col", [(1, 0), (2, 3)])

    def body(i, s, t):
        def to(k):
            return t[0].at[:, start_of(i[k], cols)]

        z = i[0]
        yield None, s[0], to(0)
        yield None, s[2], to(2)
        yield z < 3, s[1], to(1)
        yield z == 3, s[4], to(1)
        yield z > 0, s[3], to(3)
        yield z == 0, s[4], to(3)

    return move(
        body, ids, [block, above, across, below, far], [shape((rows, 4 * cols))], 6
    )[0]


def normalize(ids, parts, scale, gains):
    rows, cols = scale.shape[0], parts[0].shape[1]

    def kernel(ids_ref, *refs):
        scale_ref, gain_ref, out_ref = refs[4:]
        inverse = scale_ref[:, 4:5]
        for k, place in enumerate((0, 3, 2, 1)):
            value = (refs[k][:rows].astype(F32) + scale_ref[:, k : k + 1]) * inverse
            value = value * gain_ref[k : k + 1]
            out_ref[:, start_of(ids_ref[place], cols)] = value.astype(BF16)

    return call(
        kernel, ids, [*parts, scale, gains], (), [VMEM] * 6, VMEM, shape((rows, 4 * cols))
    )


def gelu_parts(v):
    cdf = 0.5 * (1.0 + lax.erf(v * 0.7071067811865476))
    return v * cdf, cdf + v * jnp.exp(-0.5 * v * v) * 0.3989422804014327


TILE = 256


def expand(ids, rows, panel, after=()):
    hid = panel.shape[1] // 2
    steps = hid // TILE

    def kernel(ids_ref, x_ref, w_ref, hidden_ref, slope_ref):
        pre = jnp.dot(x_ref[...], w_ref[...], preferred_element_type=F32)
        act, slope = gelu_parts(pre)
        hidden_ref[...] = act.astype(BF16)
        slope_ref[...] = slope.astype(BF16)

    tile = pl.BlockSpec((rows.shape[0], TILE), lambda t, i: (0, t))
    return call(
        kernel, ids, [rows, panel], (steps,),
        [whole(rows.shape), pl.BlockSpec((C, TILE), lambda t, i: (0, i[4] * steps + t))],
        [tile, tile], [shape((rows.shape[0], hid))] * 2, after=after,
    )


def expand_grad(ids, strips, panel, slopes, after):
    rows, hid = slopes[0].shape
    steps = hid // TILE

    def kernel(ids_ref, own_ref, sib_ref, w_ref, own_slope, sib_slope, own_out, sib_out):
        for x, slope, out in ((own_ref, own_slope, own_out), (sib_ref, sib_slope, sib_out)):
            back = jnp.dot(x[...], w_ref[...], preferred_element_type=F32)
            out[...] = (back * slope[...].astype(F32)).astype(BF16)

    tile = pl.BlockSpec((rows, TILE), lambda t, i: (0, t))
    return call(
        kernel, ids, [*strips, panel, *slopes], (steps,),
        [
            whole(strips[0].shape),
            whole(strips[1].shape),
            pl.BlockSpec((C, TILE), lambda t, i: (0, i[4] * steps + t)),
            tile,
            tile,
        ],
        [tile, tile], [shape((rows, hid))] * 2, after=after,
    )


def weight_grad(ids, own, sib, right, after=()):
    rows = own.shape[0]
    hid = right[0].shape[1]
    size = C // 4

    def kernel(ids_ref, own_ref, sib_ref, own_right, sib_right, out_ref):
        acc = lax.dot_general(own_ref[...], own_right[...], FIRST, preferred_element_type=F32)
        acc += lax.dot_general(sib_ref[...], sib_right[...], FIRST, preferred_element_type=F32)
        out_ref[...] = acc.astype(BF16)

    cut = pl.BlockSpec((rows, size), lambda t, i: (0, t))
    return call(
        kernel, ids, [own, sib, *right], (4,), [cut, cut] + [whole((rows, hid))] * 2,
        pl.BlockSpec((size, hid), lambda t, i: (t, 0)), shape((C, hid)), after=after,
    )


def contract(ids, left, panel, other=None, after=()):
    rows, hid = left.shape

    def kernel(ids_ref, x_ref, w_ref, *refs):
        acc = lax.dot_general(x_ref[...], w_ref[...], LAST, preferred_element_type=F32)
        if other is not None:
            acc = acc + refs[0][...].astype(F32)
        refs[-1][...] = acc.astype(BF16)

    cut = pl.BlockSpec((rows, 512), lambda t, i: (0, t))
    more = [] if other is None else [other]
    return call(
        kernel, ids, [left, panel, *more], (C // 512,),
        [whole((rows, hid)), pl.BlockSpec((512, hid), lambda t, i: (t, i[4]))] + [cut] * len(more),
        cut, shape((rows, C)), after=after,
    )


def contract_own(ids, left, panel, other, after=()):
    rows, hid = left.shape

    def kernel(ids_ref, x_ref, w_ref, o_ref, *outs):
        acc = lax.dot_general(x_ref[...], w_ref[...], LAST, preferred_element_type=F32)
        acc = (acc + o_ref[...].astype(F32)).astype(BF16)
        for k in range(4):
            @pl.when(pl.program_id(0) == k)
            def _():
                outs[k][...] = acc

    return call(
        kernel, ids, [left, panel, other], (4,),
        [
            whole((rows, hid)),
            pl.BlockSpec((512, hid), lambda t, i: (i[t], i[4])),
            pl.BlockSpec((rows, 512), lambda t, i: (0, i[t])),
        ],
        [whole((rows, 512))] * 4, [shape((rows, 512))] * 4, after=after,
    )


def give_rows(ids, block, after):
    rows, cols = block.shape

    def body(i, s, t):
        yield None, s[0].at[start_of(1 - i[4], rows // 2)], t[0]

    return move(body, ids, [block], [shape((rows // 2, cols))], 1, after)[0]


def own_rows(ids, block, after=()):
    rows, cols = block.shape
    other = lax.ppermute(give_rows(ids, block, after), "row", SIBLING)

    def body(i, s, t):
        yield None, s[0].at[start_of(i[4], rows // 2)], t[0].at[:, start_of(i[4], cols)]
        yield None, s[1], t[0].at[:, start_of(1 - i[4], cols)]

    return move(body, ids, [block, other], [shape((rows // 2, 2 * cols))], 2)[0]


def taps(ids, low, mid, high, dw_kernel, flipped, extra=None, after=()):
    images, rows, width, chans = mid.shape
    lanes = 128
    edge = 8

    def kernel(ids_ref, *refs):
        low_ref, mid_ref, high_ref, dw_ref = refs[:4]
        outs, pad_ref = refs[4 + (extra is not None) : -1], refs[-1]
        pad_ref[:, :edge] = jnp.zeros((rows + 2 * REACH, edge, lanes), F32)
        pad_ref[:, edge + width :] = jnp.zeros((rows + 2 * REACH, edge, lanes), F32)

        @pl.loop(0, chans // lanes)
        def _(chunk):
            lane = start_of(chunk, lanes)
            pad_ref[:REACH, edge : edge + width] = low_ref[0, :, :, lane].astype(F32)
            pad_ref[REACH : REACH + rows, edge : edge + width] = mid_ref[0, :, :, lane].astype(F32)
            pad_ref[REACH + rows :, edge : edge + width] = high_ref[0, :, :, lane].astype(F32)
            totals = [jnp.zeros((width, lanes), F32)] * rows
            for off_col in range(KS):
                tap_col = KS - 1 - off_col if flipped else off_col
                for place in range(rows + 2 * REACH):
                    line = pad_ref[place, pl.ds(edge - REACH + off_col, width)]
                    for row in range(rows):
                        off_row = place - row
                        if 0 <= off_row < KS:
                            tap_row = KS - 1 - off_row if flipped else off_row
                            totals[row] += dw_ref[pl.ds(tap_row * KS + tap_col, 1), lane] * line
            for row in range(rows):
                if extra is None:
                    outs[0][0, row, :, lane] = totals[row]
                else:
                    total = refs[4][0, row, :, lane].astype(F32) + totals[row]
                    outs[0][0, row, :, lane] = total.astype(BF16)

        if extra is None:
            for row in range(rows):
                value = outs[0][0, row]
                mean = jnp.sum(value, axis=1, keepdims=True) * (1.0 / chans)
                value = value - mean
                outs[0][0, row] = value
                outs[1][0, row] = value.astype(BF16)
                outs[2][0, row] = mean
                outs[3][0, row] = jnp.sum(value * value, axis=1, keepdims=True)

    def strip(count, last=chans):
        return pl.BlockSpec((1, count, width, last), lambda b, i: (b, 0, 0, 0))

    arrays = [low, mid, high, dw_kernel.reshape(KS * KS, chans)]
    ins = [strip(REACH), strip(rows), strip(REACH), whole((KS * KS, chans))]
    if extra is None:
        thin = shape((images, rows, width, 1), F32)
        outs = [strip(rows), strip(rows), strip(rows, 1), strip(rows, 1)]
        shapes = [shape(mid.shape, F32), shape(mid.shape), thin, thin]
    else:
        arrays.append(extra)
        ins.append(strip(rows))
        outs, shapes = strip(rows), shape(mid.shape)
    return call(
        kernel, ids, arrays, (images,), ins, outs, shapes,
        [pltpu.VMEM((rows + 2 * REACH, width + 2 * edge, lanes), F32)], after,
    )


def rims(block):
    count = lax.axis_size("row")
    forward = [(i, i + 1) for i in range(count - 1)]
    backward = [(i + 1, i) for i in range(count - 1)]
    low = lax.ppermute(block[:, -REACH:], "row", forward)
    high = lax.ppermute(block[:, :REACH], "row", backward)
    return low, high


def split(row):
    high = lax.reduce_precision(row, 8, 7)
    mid = lax.reduce_precision(row - high, 8, 7)
    return [part.astype(BF16) for part in (high, mid, row - high - mid)]


def joined(rows):
    return rows[0].astype(F32) + rows[1].astype(F32) + rows[2].astype(F32)


def shifted(array, step):
    count = lax.axis_size("col")
    return lax.ppermute(array, "col", [(i, (i + step) % count) for i in range(count)])


def added(blocks):
    total = blocks[0].astype(F32)
    for block in blocks[1:]:
        total = total + block.astype(F32)
    return total


def row_scatter(whole_rows):
    return lax.psum_scatter(
        whole_rows, "row", scatter_dimension=0, tiled=True, axis_index_groups=SAME_CORE
    )


def on_device(images, dw_kernel, norm_gain, proj_in, proj_out, layer_scale, cotangent):
    local_ch = images.shape[3]
    pixels = images.shape[0] * images.shape[1] * images.shape[2]
    ids = make_ids()

    def swap(block):
        return lax.ppermute(block, "row", SIBLING)

    in_panel = lax.all_gather(proj_in, "row", axis=0, tiled=True)
    out_panel = lax.all_gather(proj_out, "row", axis=0, tiled=True)
    cot_flat = cotangent.reshape(pixels, local_ch).astype(F32)
    grad_branch = (cot_flat * layer_scale).astype(BF16)
    grad_parts = col_send(grad_branch)
    low, high = rims(images)
    centred, rounded, own_mean, own_square = taps(
        ids, low, images, high, dw_kernel, False, after=[grad_parts[1], grad_parts[3]]
    )
    centred = centred.reshape(pixels, local_ch)
    stats = [own_mean.reshape(pixels), own_square.reshape(pixels), norm_gain]
    extra = jnp.stack(split(stats[0]) + split(stats[1]) + split(stats[2]))
    extra = jnp.pad(extra, ((0, 16 - extra.shape[0]), (0, 0)))
    rounded = jnp.concatenate([rounded.reshape(pixels, local_ch), extra])
    parts = [rounded] + [shifted(rounded, step) for step in (1, 2, 3)]
    grad_own = col_gather(ids, grad_parts, before_far=[rounded])
    grad_sib = swap(grad_own)

    means, squares, gains = (
        jnp.stack([stats[k]] + [joined(part[pixels + 3 * k :]) for part in parts[1:]])
        for k in range(3)
    )
    row_mean = jnp.mean(means, axis=0)
    shifts = means - row_mean
    squares = squares + local_ch * (shifts * shifts)
    inv_std = lax.rsqrt(jnp.sum(squares, axis=0) / C + 1e-06)
    scale = jnp.concatenate([shifts, inv_std[None]]).T
    normed = (centred + shifts[0][:, None]) * inv_std[:, None]
    in_own = normalize(ids, parts, later(ids, scale, [grad_own]), gains)
    in_sib = swap(in_own)

    hidden_own, slope_own = expand(ids, in_own, in_panel)
    hidden_sib, slope_sib = expand(ids, in_sib, in_panel, [hidden_own])
    hidden = hidden_own, hidden_sib
    out_part = weight_grad(ids, grad_own, grad_sib, hidden)
    out_rows = row_scatter(out_part)
    grad_pre = expand_grad(
        ids, (grad_own, grad_sib), out_panel, (slope_own, slope_sib), [out_part]
    )
    back_give = contract(ids, grad_pre[1], in_panel)
    back_sib = swap(back_give)
    in_part = weight_grad(ids, in_own, in_sib, grad_pre, [back_give])
    in_rows = row_scatter(in_part)
    branch_give = contract(ids, hidden_sib, out_panel, None, [in_part])
    branch_sib = swap(branch_give)
    back = contract_own(ids, grad_pre[0], in_panel, back_sib, [branch_give])
    back_sent = [shifted(back[step], step) for step in (1, 2, 3)]
    branch = contract_own(ids, hidden_own, out_panel, branch_sib, [back[0]])
    back_sent[0] = later(ids, back_sent[0], [branch[0], *back_sent[1:]])
    grad_scaled = added([back[0], *back_sent])
    weighted = grad_scaled * norm_gain
    sums = jnp.stack([jnp.sum(weighted, axis=1), jnp.sum(weighted * normed, axis=1)])
    sums = sums + shifted(sums, 1) + shifted(sums, 2) + shifted(sums, 3)
    branch_sent = [shifted(later(ids, branch[step], [sums]), step) for step in (1, 2, 3)]
    branch = added([branch[0], *branch_sent])
    residual_in = images.reshape(pixels, local_ch).astype(F32)
    block_out = (residual_in + layer_scale * branch).astype(BF16).reshape(images.shape)
    grad_conv = inv_std[:, None] * (
        weighted - sums[0][:, None] / C - normed * sums[1][:, None] / C
    )
    grad_conv = grad_conv.astype(BF16).reshape(images.shape)
    low, high = rims(grad_conv)
    grad_images = taps(ids, low, grad_conv, high, dw_kernel, True, cotangent)
    return block_out, grad_images, own_rows(ids, in_rows, [grad_images]), own_rows(ids, out_rows)


def with_halo(block, sides, width):
    for axis, dim in sides:
        count = lax.axis_size(axis)
        forward = [(i, i + 1) for i in range(count - 1)]
        backward = [(target, source) for source, target in forward]
        low = lax.ppermute(
            lax.slice_in_dim(block, block.shape[dim] - width, None, axis=dim), axis, forward
        )
        high = lax.ppermute(lax.slice_in_dim(block, 0, width, axis=dim), axis, backward)
        block = jnp.concatenate([low, block, high], axis=dim)
    return block


def taps_sum(padded, dw_kernel, img_rows, img_cols, flipped):
    total = jnp.zeros(padded.shape[:1] + (img_rows, img_cols) + padded.shape[3:], jnp.float32)
    reach = 2 * (KS // 2)
    for tap_row in range(KS):
        for tap_col in range(KS):
            off_row = reach - tap_row if flipped else tap_row
            off_col = reach - tap_col if flipped else tap_col
            total = (
                total
                + dw_kernel[tap_row, tap_col]
                * padded[:, off_row : off_row + img_rows, off_col : off_col + img_cols, :]
            )
    return total


def gelu_slope(values):
    return (
        0.5 * (1.0 + lax.erf(values * 0.7071067811865476))
        + values * jnp.exp(-0.5 * values * values) * 0.3989422804014327
    )


def on_any_mesh(images, dw_kernel, norm_gain, proj_in, proj_out, layer_scale, cotangent):
    img_batch, strip_rows, img_cols, local_ch = images.shape
    pixels = img_batch * strip_rows * img_cols
    reach = KS // 2
    contract_last = (((1,), (1,)), ((), ()))
    contract_first = (((0,), (0,)), ((), ()))
    rimmed = with_halo(images, (("row", 1),), reach)
    padded = jnp.pad(rimmed.astype(jnp.float32), ((0, 0), (0, 0), (reach, reach), (0, 0)))
    conv_out = taps_sum(padded, dw_kernel, strip_rows, img_cols, False).reshape(pixels, local_ch)
    row_mean = lax.psum(jnp.sum(conv_out, axis=1), "col") / C
    centred = conv_out - row_mean[:, None]
    row_var = lax.psum(jnp.sum(centred * centred, axis=1), "col") / C
    inv_std = lax.rsqrt(row_var + 1e-06)
    normed = centred * inv_std[:, None]
    scaled = (normed * norm_gain).astype(jnp.bfloat16)
    full_in = lax.all_gather(scaled, "col", axis=1, tiled=True)
    in_panel = lax.all_gather(proj_in, "row", axis=0, tiled=True)
    out_panel = lax.all_gather(proj_out, "row", axis=0, tiled=True)
    hidden_pre = jnp.dot(full_in, in_panel, preferred_element_type=jnp.float32)
    hidden = jax.nn.gelu(hidden_pre, approximate=False).astype(jnp.bfloat16)
    contrib = lax.dot_general(hidden, out_panel, contract_last, preferred_element_type=jnp.float32)
    branch = lax.psum_scatter(
        contrib.astype(jnp.bfloat16), "col", scatter_dimension=1, tiled=True
    ).astype(jnp.float32)
    residual_in = images.reshape(pixels, local_ch).astype(jnp.float32)
    block_out = (residual_in + layer_scale * branch).astype(jnp.bfloat16).reshape(images.shape)
    cot_flat = cotangent.reshape(pixels, local_ch).astype(jnp.float32)
    grad_branch = (cot_flat * layer_scale).astype(jnp.bfloat16)
    full_grad = lax.all_gather(grad_branch, "col", axis=1, tiled=True)
    grad_proj_out = lax.psum_scatter(
        lax.dot_general(
            full_grad, hidden, contract_first, preferred_element_type=jnp.float32
        ).astype(jnp.bfloat16),
        "row",
        scatter_dimension=0,
        tiled=True,
    )
    grad_hidden = jnp.dot(full_grad, out_panel, preferred_element_type=jnp.float32)
    grad_pre = (grad_hidden * gelu_slope(hidden_pre)).astype(jnp.bfloat16)
    grad_proj_in = lax.psum_scatter(
        lax.dot_general(
            full_in, grad_pre, contract_first, preferred_element_type=jnp.float32
        ).astype(jnp.bfloat16),
        "row",
        scatter_dimension=0,
        tiled=True,
    )
    back_part = lax.dot_general(
        grad_pre, in_panel, contract_last, preferred_element_type=jnp.float32
    )
    grad_scaled = lax.psum_scatter(
        back_part.astype(jnp.bfloat16), "col", scatter_dimension=1, tiled=True
    ).astype(jnp.float32)
    weighted = grad_scaled * norm_gain
    sum_one, sum_two = lax.psum(
        (jnp.sum(weighted, axis=1), jnp.sum(weighted * normed, axis=1)), "col"
    )
    grad_conv = inv_std[:, None] * (weighted - sum_one[:, None] / C - normed * sum_two[:, None] / C)
    grad_conv = grad_conv.reshape(img_batch, strip_rows, img_cols, local_ch)
    grad_rim = with_halo(grad_conv.astype(jnp.bfloat16), (("row", 1),), reach).astype(
        grad_conv.dtype
    )
    grad_pad = jnp.pad(grad_rim, ((0, 0), (0, 0), (reach, reach), (0, 0)))
    input_grad = taps_sum(grad_pad, dw_kernel, strip_rows, img_cols, True)
    grad_images = (cotangent.astype(jnp.float32) + input_grad).astype(jnp.bfloat16)
    return (block_out, grad_images, grad_proj_in, grad_proj_out)


def solution(mesh):
    tuned = mesh.shape["row"] == 8 and mesh.shape["col"] == 4
    placed = (
        P(None, "row", None, "col"),
        P(None, None, "col"),
        P("col"),
        P("row", "col"),
        P("row", "col"),
        P("col"),
        P(None, "row", None, "col"),
    )
    return jax.shard_map(
        on_device if tuned else on_any_mesh,
        mesh=mesh,
        in_specs=placed,
        out_specs=(
            P(None, "row", None, "col"),
            P(None, "row", None, "col"),
            P("row", "col"),
            P("row", "col"),
        ),
        check_vma=False,
    )
```

```python
import functools

import jax
import jax.numpy as jnp
import numpy as np
from jax import lax
from jax.experimental import pallas as pl
from jax.experimental.pallas import tpu as pltpu
from jax.sharding import PartitionSpec as P

C = 2048
KS = 7
REACH = KS // 2
F32 = jnp.float32
BF16 = jnp.bfloat16
LAST = (((1,), (1,)), ((), ()))
FIRST = (((0,), (0,)), ((), ()))
CHIPS = (0, 1, 3, 2)
SIBLING = [(i, i ^ 1) for i in range(8)]
UP = [(0, 1), (1, 2), (2, 3)]
DOWN = [(1, 0), (2, 1), (3, 2)]
ACROSS = [(0, 2), (1, 3), (2, 0), (3, 1)]
SAME_CORE = [[0, 2, 4, 6], [1, 3, 5, 7]]
ANY = pl.BlockSpec(memory_space=pl.ANY)
VMEM = pl.BlockSpec(memory_space=pltpu.VMEM)
PARAMS = pltpu.CompilerParams(vmem_limit_bytes=52 * 2**20)
HINT = pl.CostEstimate(flops=0, bytes_accessed=0, transcendentals=0)
WORK = pl.CostEstimate(flops=2**32, bytes_accessed=12 * 2**20, transcendentals=0)


def ring_pairs(sense):
    pairs = []
    for place, chip in enumerate(CHIPS):
        for core in (0, 1):
            step = sense if core == 0 else -sense
            pairs.append((2 * chip + core, 2 * CHIPS[(place + step) % 4] + core))
    return pairs


AHEAD = ring_pairs(1)
BEHIND = ring_pairs(-1)


def shape(dims, dtype=BF16):
    return jax.ShapeDtypeStruct(dims, dtype)


def call(
    body, ids, arrays, grid, ins, outs, shapes, scratch=(), after=(), aliases=None
):
    count = len(arrays)

    def kernel(ids_ref, *refs):
        body(ids_ref, *refs[:count], *refs[count + len(after) :])

    return pl.pallas_call(
        kernel,
        grid_spec=pltpu.PrefetchScalarGridSpec(
            num_scalar_prefetch=1,
            grid=grid,
            in_specs=list(ins) + [ANY] * len(after),
            out_specs=outs,
            scratch_shapes=scratch,
        ),
        out_shape=shapes,
        compiler_params=PARAMS,
        cost_estimate=WORK if grid else HINT,
        input_output_aliases=aliases or {},
    )(ids, *arrays, *after)


def later(ids, array, after):
    return call(
        lambda *refs: None, ids, [array], (), [ANY], ANY, shape(array.shape, array.dtype),
        after=after, aliases={1: 0},
    )


def whole(dims):
    return pl.BlockSpec(dims, lambda *_: (0,) * len(dims))


def make_ids():
    table = np.zeros((8, 4, 9), np.int32)
    for row in range(8):
        place, sense = CHIPS.index(row // 2), 1 - 2 * (row % 2)
        ring = [CHIPS[(place + sense * step) % 4] for step in (0, -1, 1, 2)]
        for z in range(4):
            table[row, z] = [z, (z + 1) % 4, (z + 2) % 4, (z + 3) % 4, row % 2] + ring
    place = (lax.axis_index("row"), lax.axis_index("col"), 0)
    return lax.dynamic_slice(jnp.asarray(table), place, (1, 1, 9)).reshape(9)


def move(body, ids, arrays, shapes, count, after=()):
    def kernel(ids_ref, *refs):
        sems = refs[-1]
        pairs = list(body(ids_ref, refs[: len(arrays)], refs[len(arrays) : -1]))
        copies = [pltpu.make_async_copy(src, dst, sems.at[i]) for i, (_, src, dst) in enumerate(pairs)]
        for (when, _, _), copy in zip(pairs, copies):
            if when is None:
                copy.start()
            else:
                pl.when(when)(copy.start)
        for (when, _, _), copy in zip(pairs, copies):
            if when is None:
                copy.wait()
            else:
                pl.when(when)(copy.wait)

    return call(
        kernel, ids, arrays, (), [ANY] * len(arrays), [VMEM] * len(shapes), shapes,
        [pltpu.SemaphoreType.DMA((count,))], after,
    )


def start_of(index, size):
    return pl.ds(pl.multiple_of(index * size, size), size)


def col_send(block):
    across = lax.ppermute(block, "col", ACROSS)
    above = lax.ppermute(block, "col", DOWN)
    below = lax.ppermute(block, "col", UP)
    return block, above, across, below


def col_gather(ids, parts, before_far):
    block, above, across, below = parts
    rows, cols = block.shape
    across = later(ids, across, before_far)
    far = lax.ppermute(across, "col", [(1, 0), (2, 3)])

    def body(i, s, t):
        def to(k):
            return t[0].at[:, start_of(i[k], cols)]

        z = i[0]
        yield None, s[0], to(0)
        yield None, s[2], to(2)
        yield z < 3, s[1], to(1)
        yield z == 3, s[4], to(1)
        yield z > 0, s[3], to(3)
        yield z == 0, s[4], to(3)

    return move(
        body, ids, [block, above, across, below, far], [shape((rows, 4 * cols))], 6
    )[0]


def normalize(ids, parts, scale, gains):
    rows, cols = scale.shape[0], parts[0].shape[1]

    def kernel(ids_ref, *refs):
        scale_ref, gain_ref, out_ref = refs[4:]
        inverse = scale_ref[:, 4:5]
        for k, place in enumerate((0, 3, 2, 1)):
            value = (refs[k][:rows].astype(F32) + scale_ref[:, k : k + 1]) * inverse
            value = value * gain_ref[k : k + 1]
            out_ref[:, start_of(ids_ref[place], cols)] = value.astype(BF16)

    return call(
        kernel, ids, [*parts, scale, gains], (), [VMEM] * 6, VMEM, shape((rows, 4 * cols))
    )


def gelu_parts(v):
    cdf = 0.5 * (1.0 + lax.erf(v * 0.7071067811865476))
    return v * cdf, cdf + v * jnp.exp(-0.5 * v * v) * 0.3989422804014327


TILE = 256


def expand(ids, rows, panel, after=()):
    hid = panel.shape[1] // 2
    steps = hid // TILE

    def kernel(ids_ref, x_ref, w_ref, hidden_ref, slope_ref):
        pre = jnp.dot(x_ref[...], w_ref[...], preferred_element_type=F32)
        act, slope = gelu_parts(pre)
        hidden_ref[...] = act.astype(BF16)
        slope_ref[...] = slope.astype(BF16)

    tile = pl.BlockSpec((rows.shape[0], TILE), lambda t, i: (0, t))
    return call(
        kernel, ids, [rows, panel], (steps,),
        [whole(rows.shape), pl.BlockSpec((C, TILE), lambda t, i: (0, i[4] * steps + t))],
        [tile, tile], [shape((rows.shape[0], hid))] * 2, after=after,
    )


def expand_grad(ids, strips, panel, slopes, after):
    rows, hid = slopes[0].shape
    steps = hid // TILE

    def kernel(ids_ref, own_ref, sib_ref, w_ref, own_slope, sib_slope, own_out, sib_out):
        for x, slope, out in ((own_ref, own_slope, own_out), (sib_ref, sib_slope, sib_out)):
            back = jnp.dot(x[...], w_ref[...], preferred_element_type=F32)
            out[...] = (back * slope[...].astype(F32)).astype(BF16)

    tile = pl.BlockSpec((rows, TILE), lambda t, i: (0, t))
    return call(
        kernel, ids, [*strips, panel, *slopes], (steps,),
        [
            whole(strips[0].shape),
            whole(strips[1].shape),
            pl.BlockSpec((C, TILE), lambda t, i: (0, i[4] * steps + t)),
            tile,
            tile,
        ],
        [tile, tile], [shape((rows, hid))] * 2, after=after,
    )


def weight_grad(ids, own, sib, right, slots, after=()):
    rows = own.shape[0]
    hid = right[0].shape[1]
    size = C // 4

    def kernel(ids_ref, own_ref, sib_ref, own_right, sib_right, *outs):
        acc = lax.dot_general(own_ref[...], own_right[...], FIRST, preferred_element_type=F32)
        acc += lax.dot_general(sib_ref[...], sib_right[...], FIRST, preferred_element_type=F32)
        if not slots:
            outs[0][...] = acc.astype(BF16)
            return
        for k in range(4):
            @pl.when(pl.program_id(0) == k)
            def _():
                outs[k][...] = acc.astype(BF16)

    if slots:
        cut = pl.BlockSpec((rows, size), lambda t, i: (0, i[8 - t]))
        outs, shapes = [whole((size, hid))] * 4, [shape((size, hid))] * 4
    else:
        cut = pl.BlockSpec((rows, size), lambda t, i: (0, t))
        outs, shapes = pl.BlockSpec((size, hid), lambda t, i: (t, 0)), shape((C, hid))
    return call(
        kernel, ids, [own, sib, *right], (4,), [cut, cut] + [whole((rows, hid))] * 2, outs, shapes,
        after=after,
    )


def contract(ids, left, panel, other=None, after=()):
    rows, hid = left.shape

    def kernel(ids_ref, x_ref, w_ref, *refs):
        acc = lax.dot_general(x_ref[...], w_ref[...], LAST, preferred_element_type=F32)
        if other is not None:
            acc = acc + refs[0][...].astype(F32)
        refs[-1][...] = acc.astype(BF16)

    cut = pl.BlockSpec((rows, 512), lambda t, i: (0, t))
    more = [] if other is None else [other]
    return call(
        kernel, ids, [left, panel, *more], (C // 512,),
        [whole((rows, hid)), pl.BlockSpec((512, hid), lambda t, i: (t, i[4]))] + [cut] * len(more),
        cut, shape((rows, C)), after=after,
    )


def contract_own(ids, left, panel, other, after=()):
    rows, hid = left.shape

    def kernel(ids_ref, x_ref, w_ref, o_ref, *outs):
        acc = lax.dot_general(x_ref[...], w_ref[...], LAST, preferred_element_type=F32)
        acc = (acc + o_ref[...].astype(F32)).astype(BF16)
        for k in range(4):
            @pl.when(pl.program_id(0) == k)
            def _():
                outs[k][...] = acc

    return call(
        kernel, ids, [left, panel, other], (4,),
        [
            whole((rows, hid)),
            pl.BlockSpec((512, hid), lambda t, i: (i[t], i[4])),
            pl.BlockSpec((rows, 512), lambda t, i: (0, i[t])),
        ],
        [whole((rows, 512))] * 4, [shape((rows, 512))] * 4, after=after,
    )


def ring_send(blocks):
    return lax.ppermute(blocks[0], "row", BEHIND), lax.ppermute(blocks[1], "row", AHEAD)


def ring_scatter(blocks, sent):
    _, _, behind, own = blocks
    one = lax.ppermute((sent[0].astype(F32) + behind.astype(F32)).astype(BF16), "row", BEHIND)
    return (own.astype(F32) + one.astype(F32) + sent[1].astype(F32)).astype(BF16)


def give_rows(ids, block, after):
    rows, cols = block.shape

    def body(i, s, t):
        yield None, s[0].at[start_of(1 - i[4], rows // 2)], t[0]

    return move(body, ids, [block], [shape((rows // 2, cols))], 1, after)[0]


def own_rows(ids, block, after=()):
    rows, cols = block.shape
    other = lax.ppermute(give_rows(ids, block, after), "row", SIBLING)

    def body(i, s, t):
        yield None, s[0].at[start_of(i[4], rows // 2)], t[0].at[:, start_of(i[4], cols)]
        yield None, s[1], t[0].at[:, start_of(1 - i[4], cols)]

    return move(body, ids, [block, other], [shape((rows // 2, 2 * cols))], 2)[0]


def taps(ids, low, mid, high, dw_kernel, flipped, extra=None, after=()):
    images, rows, width, chans = mid.shape
    lanes = 128
    edge = 8

    def kernel(ids_ref, *refs):
        low_ref, mid_ref, high_ref, dw_ref = refs[:4]
        outs, pad_ref = refs[4 + (extra is not None) : -1], refs[-1]
        pad_ref[:, :edge] = jnp.zeros((rows + 2 * REACH, edge, lanes), F32)
        pad_ref[:, edge + width :] = jnp.zeros((rows + 2 * REACH, edge, lanes), F32)

        @pl.loop(0, chans // lanes)
        def _(chunk):
            lane = start_of(chunk, lanes)
            pad_ref[:REACH, edge : edge + width] = low_ref[0, :, :, lane].astype(F32)
            pad_ref[REACH : REACH + rows, edge : edge + width] = mid_ref[0, :, :, lane].astype(F32)
            pad_ref[REACH + rows :, edge : edge + width] = high_ref[0, :, :, lane].astype(F32)
            totals = [jnp.zeros((width, lanes), F32)] * rows
            for off_col in range(KS):
                tap_col = KS - 1 - off_col if flipped else off_col
                for place in range(rows + 2 * REACH):
                    line = pad_ref[place, pl.ds(edge - REACH + off_col, width)]
                    for row in range(rows):
                        off_row = place - row
                        if 0 <= off_row < KS:
                            tap_row = KS - 1 - off_row if flipped else off_row
                            totals[row] += dw_ref[pl.ds(tap_row * KS + tap_col, 1), lane] * line
            for row in range(rows):
                if extra is None:
                    outs[0][0, row, :, lane] = totals[row]
                else:
                    total = refs[4][0, row, :, lane].astype(F32) + totals[row]
                    outs[0][0, row, :, lane] = total.astype(BF16)

        if extra is None:
            for row in range(rows):
                value = outs[0][0, row]
                mean = jnp.sum(value, axis=1, keepdims=True) * (1.0 / chans)
                value = value - mean
                outs[0][0, row] = value
                outs[1][0, row] = value.astype(BF16)
                outs[2][0, row] = mean
                outs[3][0, row] = jnp.sum(value * value, axis=1, keepdims=True)

    def strip(count, last=chans):
        return pl.BlockSpec((1, count, width, last), lambda b, i: (b, 0, 0, 0))

    arrays = [low, mid, high, dw_kernel.reshape(KS * KS, chans)]
    ins = [strip(REACH), strip(rows), strip(REACH), whole((KS * KS, chans))]
    if extra is None:
        thin = shape((images, rows, width, 1), F32)
        outs = [strip(rows), strip(rows), strip(rows, 1), strip(rows, 1)]
        shapes = [shape(mid.shape, F32), shape(mid.shape), thin, thin]
    else:
        arrays.append(extra)
        ins.append(strip(rows))
        outs, shapes = strip(rows), shape(mid.shape)
    return call(
        kernel, ids, arrays, (images,), ins, outs, shapes,
        [pltpu.VMEM((rows + 2 * REACH, width + 2 * edge, lanes), F32)], after,
    )


def rims(block):
    count = lax.axis_size("row")
    forward = [(i, i + 1) for i in range(count - 1)]
    backward = [(i + 1, i) for i in range(count - 1)]
    low = lax.ppermute(block[:, -REACH:], "row", forward)
    high = lax.ppermute(block[:, :REACH], "row", backward)
    return low, high


def split(row):
    high = lax.reduce_precision(row, 8, 7)
    mid = lax.reduce_precision(row - high, 8, 7)
    return [part.astype(BF16) for part in (high, mid, row - high - mid)]


def joined(rows):
    return rows[0].astype(F32) + rows[1].astype(F32) + rows[2].astype(F32)


def shifted(array, step):
    count = lax.axis_size("col")
    return lax.ppermute(array, "col", [(i, (i + step) % count) for i in range(count)])


def added(blocks):
    total = blocks[0].astype(F32)
    for block in blocks[1:]:
        total = total + block.astype(F32)
    return total


def row_scatter(whole_rows):
    return lax.psum_scatter(
        whole_rows, "row", scatter_dimension=0, tiled=True, axis_index_groups=SAME_CORE
    )


def on_device(images, dw_kernel, norm_gain, proj_in, proj_out, layer_scale, cotangent):
    local_ch = images.shape[3]
    pixels = images.shape[0] * images.shape[1] * images.shape[2]
    ids = make_ids()

    def swap(block):
        return lax.ppermute(block, "row", SIBLING)

    in_panel = lax.all_gather(proj_in, "row", axis=0, tiled=True)
    out_panel = lax.all_gather(proj_out, "row", axis=0, tiled=True)
    cot_flat = cotangent.reshape(pixels, local_ch).astype(F32)
    grad_branch = (cot_flat * layer_scale).astype(BF16)
    grad_parts = col_send(grad_branch)
    low, high = rims(images)
    centred, rounded, own_mean, own_square = taps(
        ids, low, images, high, dw_kernel, False, after=[grad_parts[1], grad_parts[3]]
    )
    centred = centred.reshape(pixels, local_ch)
    stats = [own_mean.reshape(pixels), own_square.reshape(pixels), norm_gain]
    extra = jnp.stack(split(stats[0]) + split(stats[1]) + split(stats[2]))
    extra = jnp.pad(extra, ((0, 16 - extra.shape[0]), (0, 0)))
    rounded = jnp.concatenate([rounded.reshape(pixels, local_ch), extra])
    parts = [rounded] + [shifted(rounded, step) for step in (1, 2, 3)]
    grad_own = col_gather(ids, grad_parts, before_far=[rounded])
    grad_sib = swap(grad_own)

    means, squares, gains = (
        jnp.stack([stats[k]] + [joined(part[pixels + 3 * k :]) for part in parts[1:]])
        for k in range(3)
    )
    row_mean = jnp.mean(means, axis=0)
    shifts = means - row_mean
    squares = squares + local_ch * (shifts * shifts)
    inv_std = lax.rsqrt(jnp.sum(squares, axis=0) / C + 1e-06)
    scale = jnp.concatenate([shifts, inv_std[None]]).T
    normed = (centred + shifts[0][:, None]) * inv_std[:, None]
    in_own = normalize(ids, parts, later(ids, scale, [grad_own]), gains)
    in_sib = swap(in_own)

    hidden_own, slope_own = expand(ids, in_own, in_panel)
    hidden_sib, slope_sib = expand(ids, in_sib, in_panel, [hidden_own])
    hidden = hidden_own, hidden_sib
    out_part = weight_grad(ids, grad_own, grad_sib, hidden, False)
    out_rows = row_scatter(out_part)
    grad_pre = expand_grad(
        ids, (grad_own, grad_sib), out_panel, (slope_own, slope_sib), [out_part]
    )
    back_give = contract(ids, grad_pre[1], in_panel)
    back_sib = swap(back_give)
    branch_give = contract(ids, hidden_sib, out_panel, None, [back_give])
    branch_sib = swap(branch_give)
    back = contract_own(ids, grad_pre[0], in_panel, back_sib, [branch_give])
    back_sent = [shifted(back[step], step) for step in (1, 2, 3)]
    contrib = contract(ids, hidden_own, out_panel, branch_sib, [back[0]])
    in_parts = weight_grad(ids, in_own, in_sib, grad_pre, True, [contrib])
    in_sent = ring_send(in_parts)
    back_sent[0] = later(ids, back_sent[0], [in_parts[0], *back_sent[1:]])
    contrib = later(ids, contrib, [back_sent[0]])
    branch = lax.psum_scatter(contrib, "col", scatter_dimension=1, tiled=True)
    in_rows = ring_scatter(in_parts, in_sent)
    seen = back_sent[0][:8, :128] + back_sent[0][8:16, :128]
    back_sent[0] = later(ids, back_sent[0], [seen, *in_sent])
    grad_scaled = added([back[0], *back_sent])
    weighted = grad_scaled * norm_gain
    sums = jnp.stack([jnp.sum(weighted, axis=1), jnp.sum(weighted * normed, axis=1)])
    sums = sums + shifted(sums, 1) + shifted(sums, 2) + shifted(sums, 3)
    grad_conv = inv_std[:, None] * (
        weighted - sums[0][:, None] / C - normed * sums[1][:, None] / C
    )
    grad_conv = grad_conv.astype(BF16).reshape(images.shape)
    low, high = rims(grad_conv)
    grad_images = taps(ids, low, grad_conv, high, dw_kernel, True, cotangent)
    grad_in, grad_out = own_rows(ids, in_rows, [grad_images]), own_rows(ids, out_rows)
    branch = later(ids, branch, [grad_in, grad_out])
    residual_in = images.reshape(pixels, local_ch).astype(F32)
    block_out = (residual_in + layer_scale * branch.astype(F32)).astype(BF16).reshape(images.shape)
    return block_out, grad_images, grad_in, grad_out


def with_halo(block, sides, width):
    for axis, dim in sides:
        count = lax.axis_size(axis)
        forward = [(i, i + 1) for i in range(count - 1)]
        backward = [(target, source) for source, target in forward]
        low = lax.ppermute(
            lax.slice_in_dim(block, block.shape[dim] - width, None, axis=dim), axis, forward
        )
        high = lax.ppermute(lax.slice_in_dim(block, 0, width, axis=dim), axis, backward)
        block = jnp.concatenate([low, block, high], axis=dim)
    return block


def taps_sum(padded, dw_kernel, img_rows, img_cols, flipped):
    total = jnp.zeros(padded.shape[:1] + (img_rows, img_cols) + padded.shape[3:], jnp.float32)
    reach = 2 * (KS // 2)
    for tap_row in range(KS):
        for tap_col in range(KS):
            off_row = reach - tap_row if flipped else tap_row
            off_col = reach - tap_col if flipped else tap_col
            total = (
                total
                + dw_kernel[tap_row, tap_col]
                * padded[:, off_row : off_row + img_rows, off_col : off_col + img_cols, :]
            )
    return total


def gelu_slope(values):
    return (
        0.5 * (1.0 + lax.erf(values * 0.7071067811865476))
        + values * jnp.exp(-0.5 * values * values) * 0.3989422804014327
    )


def on_any_mesh(images, dw_kernel, norm_gain, proj_in, proj_out, layer_scale, cotangent):
    img_batch, strip_rows, img_cols, local_ch = images.shape
    pixels = img_batch * strip_rows * img_cols
    reach = KS // 2
    contract_last = (((1,), (1,)), ((), ()))
    contract_first = (((0,), (0,)), ((), ()))
    rimmed = with_halo(images, (("row", 1),), reach)
    padded = jnp.pad(rimmed.astype(jnp.float32), ((0, 0), (0, 0), (reach, reach), (0, 0)))
    conv_out = taps_sum(padded, dw_kernel, strip_rows, img_cols, False).reshape(pixels, local_ch)
    row_mean = lax.psum(jnp.sum(conv_out, axis=1), "col") / C
    centred = conv_out - row_mean[:, None]
    row_var = lax.psum(jnp.sum(centred * centred, axis=1), "col") / C
    inv_std = lax.rsqrt(row_var + 1e-06)
    normed = centred * inv_std[:, None]
    scaled = (normed * norm_gain).astype(jnp.bfloat16)
    full_in = lax.all_gather(scaled, "col", axis=1, tiled=True)
    in_panel = lax.all_gather(proj_in, "row", axis=0, tiled=True)
    out_panel = lax.all_gather(proj_out, "row", axis=0, tiled=True)
    hidden_pre = jnp.dot(full_in, in_panel, preferred_element_type=jnp.float32)
    hidden = jax.nn.gelu(hidden_pre, approximate=False).astype(jnp.bfloat16)
    contrib = lax.dot_general(hidden, out_panel, contract_last, preferred_element_type=jnp.float32)
    branch = lax.psum_scatter(
        contrib.astype(jnp.bfloat16), "col", scatter_dimension=1, tiled=True
    ).astype(jnp.float32)
    residual_in = images.reshape(pixels, local_ch).astype(jnp.float32)
    block_out = (residual_in + layer_scale * branch.astype(F32)).astype(jnp.bfloat16).reshape(images.shape)
    cot_flat = cotangent.reshape(pixels, local_ch).astype(jnp.float32)
    grad_branch = (cot_flat * layer_scale).astype(jnp.bfloat16)
    full_grad = lax.all_gather(grad_branch, "col", axis=1, tiled=True)
    grad_proj_out = lax.psum_scatter(
        lax.dot_general(
            full_grad, hidden, contract_first, preferred_element_type=jnp.float32
        ).astype(jnp.bfloat16),
        "row",
        scatter_dimension=0,
        tiled=True,
    )
    grad_hidden = jnp.dot(full_grad, out_panel, preferred_element_type=jnp.float32)
    grad_pre = (grad_hidden * gelu_slope(hidden_pre)).astype(jnp.bfloat16)
    grad_proj_in = lax.psum_scatter(
        lax.dot_general(
            full_in, grad_pre, contract_first, preferred_element_type=jnp.float32
        ).astype(jnp.bfloat16),
        "row",
        scatter_dimension=0,
        tiled=True,
    )
    back_part = lax.dot_general(
        grad_pre, in_panel, contract_last, preferred_element_type=jnp.float32
    )
    grad_scaled = lax.psum_scatter(
        back_part.astype(jnp.bfloat16), "col", scatter_dimension=1, tiled=True
    ).astype(jnp.float32)
    weighted = grad_scaled * norm_gain
    sum_one, sum_two = lax.psum(
        (jnp.sum(weighted, axis=1), jnp.sum(weighted * normed, axis=1)), "col"
    )
    grad_conv = inv_std[:, None] * (weighted - sum_one[:, None] / C - normed * sum_two[:, None] / C)
    grad_conv = grad_conv.reshape(img_batch, strip_rows, img_cols, local_ch)
    grad_rim = with_halo(grad_conv.astype(jnp.bfloat16), (("row", 1),), reach).astype(
        grad_conv.dtype
    )
    grad_pad = jnp.pad(grad_rim, ((0, 0), (0, 0), (reach, reach), (0, 0)))
    input_grad = taps_sum(grad_pad, dw_kernel, strip_rows, img_cols, True)
    grad_images = (cotangent.astype(jnp.float32) + input_grad).astype(jnp.bfloat16)
    return (block_out, grad_images, grad_proj_in, grad_proj_out)


def solution(mesh):
    tuned = mesh.shape["row"] == 8 and mesh.shape["col"] == 4
    placed = (
        P(None, "row", None, "col"),
        P(None, None, "col"),
        P("col"),
        P("row", "col"),
        P("row", "col"),
        P("col"),
        P(None, "row", None, "col"),
    )
    return jax.shard_map(
        on_device if tuned else on_any_mesh,
        mesh=mesh,
        in_specs=placed,
        out_specs=(
            P(None, "row", None, "col"),
            P(None, "row", None, "col"),
            P("row", "col"),
            P("row", "col"),
        ),
        check_vma=False,
    )
```

```python
import functools

import jax
import jax.numpy as jnp
import numpy as np
from jax import lax
from jax.experimental import pallas as pl
from jax.experimental.pallas import tpu as pltpu
from jax.sharding import PartitionSpec as P

C = 2048
KS = 7
REACH = KS // 2
F32 = jnp.float32
BF16 = jnp.bfloat16
LAST = (((1,), (1,)), ((), ()))
FIRST = (((0,), (0,)), ((), ()))
CHIPS = (0, 1, 3, 2)
SIBLING = [(i, i ^ 1) for i in range(8)]
UP = [(0, 1), (1, 2), (2, 3)]
DOWN = [(1, 0), (2, 1), (3, 2)]
ACROSS = [(0, 2), (1, 3), (2, 0), (3, 1)]
SAME_CORE = [[0, 2, 4, 6], [1, 3, 5, 7]]
ANY = pl.BlockSpec(memory_space=pl.ANY)
VMEM = pl.BlockSpec(memory_space=pltpu.VMEM)
PARAMS = pltpu.CompilerParams(vmem_limit_bytes=46 * 2**20)
HINT = pl.CostEstimate(flops=0, bytes_accessed=0, transcendentals=0)
WORK = pl.CostEstimate(flops=2**32, bytes_accessed=12 * 2**20, transcendentals=0)


def ring_pairs(sense):
    pairs = []
    for place, chip in enumerate(CHIPS):
        for core in (0, 1):
            step = sense if core == 0 else -sense
            pairs.append((2 * chip + core, 2 * CHIPS[(place + step) % 4] + core))
    return pairs


AHEAD = ring_pairs(1)
BEHIND = ring_pairs(-1)


def shape(dims, dtype=BF16):
    return jax.ShapeDtypeStruct(dims, dtype)


def call(
    body, ids, arrays, grid, ins, outs, shapes, scratch=(), after=(), aliases=None
):
    count = len(arrays)

    def kernel(ids_ref, *refs):
        body(ids_ref, *refs[:count], *refs[count + len(after) :])

    return pl.pallas_call(
        kernel,
        grid_spec=pltpu.PrefetchScalarGridSpec(
            num_scalar_prefetch=1,
            grid=grid,
            in_specs=list(ins) + [ANY] * len(after),
            out_specs=outs,
            scratch_shapes=scratch,
        ),
        out_shape=shapes,
        compiler_params=PARAMS,
        cost_estimate=WORK if grid else HINT,
        input_output_aliases=aliases or {},
    )(ids, *arrays, *after)


def later(ids, array, after):
    return call(
        lambda *refs: None, ids, [array], (), [ANY], ANY, shape(array.shape, array.dtype),
        after=after, aliases={1: 0},
    )


def whole(dims):
    return pl.BlockSpec(dims, lambda *_: (0,) * len(dims))


def make_ids():
    table = np.zeros((8, 4, 9), np.int32)
    for row in range(8):
        place, sense = CHIPS.index(row // 2), 1 - 2 * (row % 2)
        ring = [CHIPS[(place + sense * step) % 4] for step in (0, -1, 1, 2)]
        for z in range(4):
            table[row, z] = [z, (z + 1) % 4, (z + 2) % 4, (z + 3) % 4, row % 2] + ring
    place = (lax.axis_index("row"), lax.axis_index("col"), 0)
    return lax.dynamic_slice(jnp.asarray(table), place, (1, 1, 9)).reshape(9)


def move(body, ids, arrays, shapes, count, after=()):
    def kernel(ids_ref, *refs):
        sems = refs[-1]
        pairs = list(body(ids_ref, refs[: len(arrays)], refs[len(arrays) : -1]))
        copies = [pltpu.make_async_copy(src, dst, sems.at[i]) for i, (_, src, dst) in enumerate(pairs)]
        for (when, _, _), copy in zip(pairs, copies):
            if when is None:
                copy.start()
            else:
                pl.when(when)(copy.start)
        for (when, _, _), copy in zip(pairs, copies):
            if when is None:
                copy.wait()
            else:
                pl.when(when)(copy.wait)

    return call(
        kernel, ids, arrays, (), [ANY] * len(arrays), [VMEM] * len(shapes), shapes,
        [pltpu.SemaphoreType.DMA((count,))], after,
    )


def start_of(index, size):
    return pl.ds(pl.multiple_of(index * size, size), size)


def col_send(block):
    across = lax.ppermute(block, "col", ACROSS)
    above = lax.ppermute(block, "col", DOWN)
    below = lax.ppermute(block, "col", UP)
    return block, above, across, below


def col_gather(ids, parts, before_far):
    block, above, across, below = parts
    rows, cols = block.shape
    across = later(ids, across, before_far)
    far = lax.ppermute(across, "col", [(1, 0), (2, 3)])

    def body(i, s, t):
        def to(k):
            return t[0].at[:, start_of(i[k], cols)]

        z = i[0]
        yield None, s[0], to(0)
        yield None, s[2], to(2)
        yield z < 3, s[1], to(1)
        yield z == 3, s[4], to(1)
        yield z > 0, s[3], to(3)
        yield z == 0, s[4], to(3)

    return move(
        body, ids, [block, above, across, below, far], [shape((rows, 4 * cols))], 6
    )[0]


def normalize(ids, parts, scale, gains):
    rows, cols = scale.shape[0], parts[0].shape[1]

    def kernel(ids_ref, *refs):
        scale_ref, gain_ref, out_ref = refs[4:]
        inverse = scale_ref[:, 4:5]
        for k, place in enumerate((0, 3, 2, 1)):
            value = (refs[k][:rows].astype(F32) + scale_ref[:, k : k + 1]) * inverse
            value = value * gain_ref[k : k + 1]
            out_ref[:, start_of(ids_ref[place], cols)] = value.astype(BF16)

    return call(
        kernel, ids, [*parts, scale, gains], (), [VMEM] * 6, VMEM, shape((rows, 4 * cols))
    )


def gelu_parts(v):
    cdf = 0.5 * (1.0 + lax.erf(v * 0.7071067811865476))
    return v * cdf, cdf + v * jnp.exp(-0.5 * v * v) * 0.3989422804014327


TILE = 512


def expand(ids, rows, panel, after=()):
    hid = panel.shape[1] // 2
    steps = hid // TILE

    def kernel(ids_ref, x_ref, w_ref, hidden_ref, slope_ref):
        pre = jnp.dot(x_ref[...], w_ref[...], preferred_element_type=F32)
        act, slope = gelu_parts(pre)
        hidden_ref[...] = act.astype(BF16)
        slope_ref[...] = slope.astype(BF16)

    tile = pl.BlockSpec((rows.shape[0], TILE), lambda t, i: (0, t))
    return call(
        kernel, ids, [rows, panel], (steps,),
        [whole(rows.shape), pl.BlockSpec((C, TILE), lambda t, i: (0, i[4] * steps + t))],
        [tile, tile], [shape((rows.shape[0], hid))] * 2, after=after,
    )


def expand_grad(ids, strip, panel, slope, after):
    rows, hid = slope.shape
    steps = hid // TILE

    def kernel(ids_ref, x_ref, w_ref, slope_ref, out_ref):
        back = jnp.dot(x_ref[...], w_ref[...], preferred_element_type=F32)
        out_ref[...] = (back * slope_ref[...].astype(F32)).astype(BF16)

    tile = pl.BlockSpec((rows, TILE), lambda t, i: (0, t))
    return call(
        kernel, ids, [strip, panel, slope], (steps,),
        [
            whole(strip.shape),
            pl.BlockSpec((C, TILE), lambda t, i: (0, i[4] * steps + t)),
            tile,
        ],
        tile, shape((rows, hid)), after=after,
    )


def weight_grad(ids, own, sib, right, slots, after=()):
    rows = own.shape[0]
    hid = right[0].shape[1]
    size = C // 4

    def kernel(ids_ref, own_ref, sib_ref, own_right, sib_right, *outs):
        acc = lax.dot_general(own_ref[...], own_right[...], FIRST, preferred_element_type=F32)
        acc += lax.dot_general(sib_ref[...], sib_right[...], FIRST, preferred_element_type=F32)
        if not slots:
            outs[0][...] = acc.astype(BF16)
            return
        for k in range(4):
            @pl.when(pl.program_id(0) == k)
            def _():
                outs[k][...] = acc.astype(BF16)

    if slots:
        cut = pl.BlockSpec((rows, size), lambda t, i: (0, i[8 - t]))
        outs, shapes = [whole((size, hid))] * 4, [shape((size, hid))] * 4
    else:
        cut = pl.BlockSpec((rows, size), lambda t, i: (0, t))
        outs, shapes = pl.BlockSpec((size, hid), lambda t, i: (t, 0)), shape((C, hid))
    return call(
        kernel, ids, [own, sib, *right], (4,), [cut, cut] + [whole((rows, hid))] * 2, outs, shapes,
        after=after,
    )


def contract(ids, left, panel, other=None, after=()):
    rows, hid = left.shape

    def kernel(ids_ref, x_ref, w_ref, *refs):
        acc = lax.dot_general(x_ref[...], w_ref[...], LAST, preferred_element_type=F32)
        if other is not None:
            acc = acc + refs[0][...].astype(F32)
        refs[-1][...] = acc.astype(BF16)

    cut = pl.BlockSpec((rows, 1024), lambda t, i: (0, t))
    more = [] if other is None else [other]
    return call(
        kernel, ids, [left, panel, *more], (C // 1024,),
        [whole((rows, hid)), pl.BlockSpec((1024, hid), lambda t, i: (t, i[4]))] + [cut] * len(more),
        cut, shape((rows, C)), after=after,
    )


def contract_own(ids, left, panel, other, after=()):
    rows, hid = left.shape

    def kernel(ids_ref, x_ref, w_ref, o_ref, *outs):
        acc = lax.dot_general(x_ref[...], w_ref[...], LAST, preferred_element_type=F32)
        acc = (acc + o_ref[...].astype(F32)).astype(BF16)
        for k in range(4):
            @pl.when(pl.program_id(0) == k)
            def _():
                outs[k][...] = acc

    return call(
        kernel, ids, [left, panel, other], (4,),
        [
            whole((rows, hid)),
            pl.BlockSpec((512, hid), lambda t, i: (i[t], i[4])),
            pl.BlockSpec((rows, 512), lambda t, i: (0, i[t])),
        ],
        [whole((rows, 512))] * 4, [shape((rows, 512))] * 4, after=after,
    )


def ring_send(blocks):
    return lax.ppermute(blocks[0], "row", BEHIND), lax.ppermute(blocks[1], "row", AHEAD)


def ring_scatter(blocks, sent):
    _, _, behind, own = blocks
    one = lax.ppermute((sent[0].astype(F32) + behind.astype(F32)).astype(BF16), "row", BEHIND)
    return (own.astype(F32) + one.astype(F32) + sent[1].astype(F32)).astype(BF16)


def give_rows(ids, block, after):
    rows, cols = block.shape

    def body(i, s, t):
        yield None, s[0].at[start_of(1 - i[4], rows // 2)], t[0]

    return move(body, ids, [block], [shape((rows // 2, cols))], 1, after)[0]


def own_rows(ids, block, after=()):
    rows, cols = block.shape
    other = lax.ppermute(give_rows(ids, block, after), "row", SIBLING)

    def body(i, s, t):
        yield None, s[0].at[start_of(i[4], rows // 2)], t[0].at[:, start_of(i[4], cols)]
        yield None, s[1], t[0].at[:, start_of(1 - i[4], cols)]

    return move(body, ids, [block, other], [shape((rows // 2, 2 * cols))], 2)[0]


def taps(ids, low, mid, high, dw_kernel, flipped, extra=None, after=()):
    images, rows, width, chans = mid.shape
    lanes = 128
    edge = 8

    def kernel(ids_ref, *refs):
        low_ref, mid_ref, high_ref, dw_ref = refs[:4]
        outs, pad_ref = refs[4 + (extra is not None) : -1], refs[-1]
        pad_ref[:, :edge] = jnp.zeros((rows + 2 * REACH, edge, lanes), F32)
        pad_ref[:, edge + width :] = jnp.zeros((rows + 2 * REACH, edge, lanes), F32)

        @pl.loop(0, chans // lanes)
        def _(chunk):
            lane = start_of(chunk, lanes)
            pad_ref[:REACH, edge : edge + width] = low_ref[0, :, :, lane].astype(F32)
            pad_ref[REACH : REACH + rows, edge : edge + width] = mid_ref[0, :, :, lane].astype(F32)
            pad_ref[REACH + rows :, edge : edge + width] = high_ref[0, :, :, lane].astype(F32)
            totals = [jnp.zeros((width, lanes), F32)] * rows
            for off_col in range(KS):
                tap_col = KS - 1 - off_col if flipped else off_col
                for place in range(rows + 2 * REACH):
                    line = pad_ref[place, pl.ds(edge - REACH + off_col, width)]
                    for row in range(rows):
                        off_row = place - row
                        if 0 <= off_row < KS:
                            tap_row = KS - 1 - off_row if flipped else off_row
                            totals[row] += dw_ref[pl.ds(tap_row * KS + tap_col, 1), lane] * line
            for row in range(rows):
                if extra is None:
                    outs[0][0, row, :, lane] = totals[row]
                else:
                    total = refs[4][0, row, :, lane].astype(F32) + totals[row]
                    outs[0][0, row, :, lane] = total.astype(BF16)

        if extra is None:
            for row in range(rows):
                value = outs[0][0, row]
                mean = jnp.sum(value, axis=1, keepdims=True) * (1.0 / chans)
                value = value - mean
                outs[0][0, row] = value
                outs[1][0, row] = value.astype(BF16)
                outs[2][0, row] = mean
                outs[3][0, row] = jnp.sum(value * value, axis=1, keepdims=True)

    def strip(count, last=chans):
        return pl.BlockSpec((1, count, width, last), lambda b, i: (b, 0, 0, 0))

    arrays = [low, mid, high, dw_kernel.reshape(KS * KS, chans)]
    ins = [strip(REACH), strip(rows), strip(REACH), whole((KS * KS, chans))]
    if extra is None:
        thin = shape((images, rows, width, 1), F32)
        outs = [strip(rows), strip(rows), strip(rows, 1), strip(rows, 1)]
        shapes = [shape(mid.shape, F32), shape(mid.shape), thin, thin]
    else:
        arrays.append(extra)
        ins.append(strip(rows))
        outs, shapes = strip(rows), shape(mid.shape)
    return call(
        kernel, ids, arrays, (images,), ins, outs, shapes,
        [pltpu.VMEM((rows + 2 * REACH, width + 2 * edge, lanes), F32)], after,
    )


def rims(block):
    count = lax.axis_size("row")
    forward = [(i, i + 1) for i in range(count - 1)]
    backward = [(i + 1, i) for i in range(count - 1)]
    low = lax.ppermute(block[:, -REACH:], "row", forward)
    high = lax.ppermute(block[:, :REACH], "row", backward)
    return low, high


def split(row):
    high = lax.reduce_precision(row, 8, 7)
    mid = lax.reduce_precision(row - high, 8, 7)
    return [part.astype(BF16) for part in (high, mid, row - high - mid)]


def joined(rows):
    return rows[0].astype(F32) + rows[1].astype(F32) + rows[2].astype(F32)


def shifted(array, step):
    count = lax.axis_size("col")
    return lax.ppermute(array, "col", [(i, (i + step) % count) for i in range(count)])


def residual(ids, images, layer_scale, branch, after):
    rows, chans = images.shape

    def kernel(ids_ref, images_ref, scale_ref, branch_ref, out_ref):
        value = images_ref[...].astype(F32) + scale_ref[...] * branch_ref[...].astype(F32)
        out_ref[...] = value.astype(BF16)

    cut = pl.BlockSpec((rows // 2, chans), lambda t, i: (t, 0))
    return call(
        kernel, ids, [images, layer_scale.reshape(1, chans), branch], (2,),
        [cut, whole((1, chans)), cut], cut, shape((rows, chans)), after=after,
    )


def added(blocks):
    total = blocks[0].astype(F32)
    for block in blocks[1:]:
        total = total + block.astype(F32)
    return total


def row_scatter(whole_rows):
    return lax.psum_scatter(
        whole_rows, "row", scatter_dimension=0, tiled=True, axis_index_groups=SAME_CORE
    )


def on_device(images, dw_kernel, norm_gain, proj_in, proj_out, layer_scale, cotangent):
    local_ch = images.shape[3]
    pixels = images.shape[0] * images.shape[1] * images.shape[2]
    ids = make_ids()

    def swap(block):
        return lax.ppermute(block, "row", SIBLING)

    in_panel = lax.all_gather(proj_in, "row", axis=0, tiled=True)
    out_panel = lax.all_gather(proj_out, "row", axis=0, tiled=True)
    cot_flat = cotangent.reshape(pixels, local_ch).astype(F32)
    grad_branch = (cot_flat * layer_scale).astype(BF16)
    grad_parts = col_send(grad_branch)
    low, high = rims(images)
    centred, rounded, own_mean, own_square = taps(
        ids, low, images, high, dw_kernel, False, after=[grad_parts[1], grad_parts[3]]
    )
    centred = centred.reshape(pixels, local_ch)
    stats = [own_mean.reshape(pixels), own_square.reshape(pixels), norm_gain]
    extra = jnp.stack(split(stats[0]) + split(stats[1]) + split(stats[2]))
    extra = jnp.pad(extra, ((0, 16 - extra.shape[0]), (0, 0)))
    rounded = jnp.concatenate([rounded.reshape(pixels, local_ch), extra])
    parts = [rounded] + [shifted(rounded, step) for step in (1, 2, 3)]
    grad_own = col_gather(ids, grad_parts, before_far=[rounded])
    grad_sib = swap(grad_own)

    means, squares, gains = (
        jnp.stack([stats[k]] + [joined(part[pixels + 3 * k :]) for part in parts[1:]])
        for k in range(3)
    )
    row_mean = jnp.mean(means, axis=0)
    shifts = means - row_mean
    squares = squares + local_ch * (shifts * shifts)
    inv_std = lax.rsqrt(jnp.sum(squares, axis=0) / C + 1e-06)
    scale = jnp.concatenate([shifts, inv_std[None]]).T
    normed = (centred + shifts[0][:, None]) * inv_std[:, None]
    in_own = normalize(ids, parts, later(ids, scale, [grad_own]), gains)
    in_sib = swap(in_own)

    hidden_own, slope_own = expand(ids, in_own, in_panel)
    hidden_sib, slope_sib = expand(ids, in_sib, in_panel, [hidden_own])
    hidden = hidden_own, hidden_sib
    out_part = weight_grad(ids, grad_own, grad_sib, hidden, False)
    out_rows = row_scatter(out_part)
    pre_sib = expand_grad(ids, grad_sib, out_panel, slope_sib, [out_part])
    back_give = contract(ids, pre_sib, in_panel)
    back_sib = swap(back_give)
    pre_own = expand_grad(ids, grad_own, out_panel, slope_own, [back_give])
    back = contract_own(ids, pre_own, in_panel, back_sib)
    back_sent = [shifted(back[step], step) for step in (1, 2, 3)]
    branch_give = contract(ids, hidden_sib, out_panel, None, [back[0]])
    branch_sib = swap(branch_give)
    contrib = contract(ids, hidden_own, out_panel, branch_sib, [back[0]])
    in_parts = weight_grad(ids, in_own, in_sib, (pre_own, pre_sib), True, [contrib])
    in_sent = ring_send(in_parts)
    back_sent[0] = later(ids, back_sent[0], [in_parts[0], *back_sent[1:]])
    contrib = later(ids, contrib, [back_sent[0]])
    branch = lax.psum_scatter(contrib, "col", scatter_dimension=1, tiled=True)
    in_rows = ring_scatter(in_parts, in_sent)
    seen = back_sent[0][:8, :128] + back_sent[0][8:16, :128]
    back_sent[0] = later(ids, back_sent[0], [seen, *in_sent])
    grad_scaled = added([back[0], *back_sent])
    weighted = grad_scaled * norm_gain
    sums = jnp.stack([jnp.sum(weighted, axis=1), jnp.sum(weighted * normed, axis=1)])
    sums = sums + shifted(sums, 1) + shifted(sums, 2) + shifted(sums, 3)
    grad_conv = inv_std[:, None] * (
        weighted - sums[0][:, None] / C - normed * sums[1][:, None] / C
    )
    grad_conv = grad_conv.astype(BF16).reshape(images.shape)
    low, high = rims(grad_conv)
    grad_images = taps(ids, low, grad_conv, high, dw_kernel, True, cotangent)
    grad_in, grad_out = own_rows(ids, in_rows, [grad_images]), own_rows(ids, out_rows)
    flat = images.reshape(pixels, local_ch)
    block_out = residual(ids, flat, layer_scale, branch, [grad_in, grad_out]).reshape(images.shape)
    return block_out, grad_images, grad_in, grad_out


def with_halo(block, sides, width):
    for axis, dim in sides:
        count = lax.axis_size(axis)
        forward = [(i, i + 1) for i in range(count - 1)]
        backward = [(target, source) for source, target in forward]
        low = lax.ppermute(
            lax.slice_in_dim(block, block.shape[dim] - width, None, axis=dim), axis, forward
        )
        high = lax.ppermute(lax.slice_in_dim(block, 0, width, axis=dim), axis, backward)
        block = jnp.concatenate([low, block, high], axis=dim)
    return block


def taps_sum(padded, dw_kernel, img_rows, img_cols, flipped):
    total = jnp.zeros(padded.shape[:1] + (img_rows, img_cols) + padded.shape[3:], jnp.float32)
    reach = 2 * (KS // 2)
    for tap_row in range(KS):
        for tap_col in range(KS):
            off_row = reach - tap_row if flipped else tap_row
            off_col = reach - tap_col if flipped else tap_col
            total = (
                total
                + dw_kernel[tap_row, tap_col]
                * padded[:, off_row : off_row + img_rows, off_col : off_col + img_cols, :]
            )
    return total


def gelu_slope(values):
    return (
        0.5 * (1.0 + lax.erf(values * 0.7071067811865476))
        + values * jnp.exp(-0.5 * values * values) * 0.3989422804014327
    )


def on_any_mesh(images, dw_kernel, norm_gain, proj_in, proj_out, layer_scale, cotangent):
    img_batch, strip_rows, img_cols, local_ch = images.shape
    pixels = img_batch * strip_rows * img_cols
    reach = KS // 2
    contract_last = (((1,), (1,)), ((), ()))
    contract_first = (((0,), (0,)), ((), ()))
    rimmed = with_halo(images, (("row", 1),), reach)
    padded = jnp.pad(rimmed.astype(jnp.float32), ((0, 0), (0, 0), (reach, reach), (0, 0)))
    conv_out = taps_sum(padded, dw_kernel, strip_rows, img_cols, False).reshape(pixels, local_ch)
    row_mean = lax.psum(jnp.sum(conv_out, axis=1), "col") / C
    centred = conv_out - row_mean[:, None]
    row_var = lax.psum(jnp.sum(centred * centred, axis=1), "col") / C
    inv_std = lax.rsqrt(row_var + 1e-06)
    normed = centred * inv_std[:, None]
    scaled = (normed * norm_gain).astype(jnp.bfloat16)
    full_in = lax.all_gather(scaled, "col", axis=1, tiled=True)
    in_panel = lax.all_gather(proj_in, "row", axis=0, tiled=True)
    out_panel = lax.all_gather(proj_out, "row", axis=0, tiled=True)
    hidden_pre = jnp.dot(full_in, in_panel, preferred_element_type=jnp.float32)
    hidden = jax.nn.gelu(hidden_pre, approximate=False).astype(jnp.bfloat16)
    contrib = lax.dot_general(hidden, out_panel, contract_last, preferred_element_type=jnp.float32)
    branch = lax.psum_scatter(
        contrib.astype(jnp.bfloat16), "col", scatter_dimension=1, tiled=True
    ).astype(jnp.float32)
    residual_in = images.reshape(pixels, local_ch).astype(jnp.float32)
    block_out = (residual_in + layer_scale * branch.astype(F32)).astype(jnp.bfloat16).reshape(images.shape)
    cot_flat = cotangent.reshape(pixels, local_ch).astype(jnp.float32)
    grad_branch = (cot_flat * layer_scale).astype(jnp.bfloat16)
    full_grad = lax.all_gather(grad_branch, "col", axis=1, tiled=True)
    grad_proj_out = lax.psum_scatter(
        lax.dot_general(
            full_grad, hidden, contract_first, preferred_element_type=jnp.float32
        ).astype(jnp.bfloat16),
        "row",
        scatter_dimension=0,
        tiled=True,
    )
    grad_hidden = jnp.dot(full_grad, out_panel, preferred_element_type=jnp.float32)
    grad_pre = (grad_hidden * gelu_slope(hidden_pre)).astype(jnp.bfloat16)
    grad_proj_in = lax.psum_scatter(
        lax.dot_general(
            full_in, grad_pre, contract_first, preferred_element_type=jnp.float32
        ).astype(jnp.bfloat16),
        "row",
        scatter_dimension=0,
        tiled=True,
    )
    back_part = lax.dot_general(
        grad_pre, in_panel, contract_last, preferred_element_type=jnp.float32
    )
    grad_scaled = lax.psum_scatter(
        back_part.astype(jnp.bfloat16), "col", scatter_dimension=1, tiled=True
    ).astype(jnp.float32)
    weighted = grad_scaled * norm_gain
    sum_one, sum_two = lax.psum(
        (jnp.sum(weighted, axis=1), jnp.sum(weighted * normed, axis=1)), "col"
    )
    grad_conv = inv_std[:, None] * (weighted - sum_one[:, None] / C - normed * sum_two[:, None] / C)
    grad_conv = grad_conv.reshape(img_batch, strip_rows, img_cols, local_ch)
    grad_rim = with_halo(grad_conv.astype(jnp.bfloat16), (("row", 1),), reach).astype(
        grad_conv.dtype
    )
    grad_pad = jnp.pad(grad_rim, ((0, 0), (0, 0), (reach, reach), (0, 0)))
    input_grad = taps_sum(grad_pad, dw_kernel, strip_rows, img_cols, True)
    grad_images = (cotangent.astype(jnp.float32) + input_grad).astype(jnp.bfloat16)
    return (block_out, grad_images, grad_proj_in, grad_proj_out)


def solution(mesh):
    tuned = mesh.shape["row"] == 8 and mesh.shape["col"] == 4
    placed = (
        P(None, "row", None, "col"),
        P(None, None, "col"),
        P("col"),
        P("row", "col"),
        P("row", "col"),
        P("col"),
        P(None, "row", None, "col"),
    )
    return jax.shard_map(
        on_device if tuned else on_any_mesh,
        mesh=mesh,
        in_specs=placed,
        out_specs=(
            P(None, "row", None, "col"),
            P(None, "row", None, "col"),
            P("row", "col"),
            P("row", "col"),
        ),
        check_vma=False,
    )
```

```python
import functools

import jax
import jax.numpy as jnp
import numpy as np
from jax import lax
from jax.experimental import pallas as pl
from jax.experimental.pallas import tpu as pltpu
from jax.sharding import PartitionSpec as P

C = 2048
KS = 7
REACH = KS // 2
F32 = jnp.float32
BF16 = jnp.bfloat16
LAST = (((1,), (1,)), ((), ()))
FIRST = (((0,), (0,)), ((), ()))
CHIPS = (0, 1, 3, 2)
SIBLING = [(i, i ^ 1) for i in range(8)]
UP = [(0, 1), (1, 2), (2, 3)]
DOWN = [(1, 0), (2, 1), (3, 2)]
ACROSS = [(0, 2), (1, 3), (2, 0), (3, 1)]
SAME_CORE = [[0, 2, 4, 6], [1, 3, 5, 7]]
ANY = pl.BlockSpec(memory_space=pl.ANY)
VMEM = pl.BlockSpec(memory_space=pltpu.VMEM)
PARAMS = pltpu.CompilerParams(vmem_limit_bytes=46 * 2**20)
HINT = pl.CostEstimate(flops=0, bytes_accessed=0, transcendentals=0)
WORK = pl.CostEstimate(flops=2**32, bytes_accessed=12 * 2**20, transcendentals=0)


def ring_pairs(sense):
    pairs = []
    for place, chip in enumerate(CHIPS):
        for core in (0, 1):
            step = sense if core == 0 else -sense
            pairs.append((2 * chip + core, 2 * CHIPS[(place + step) % 4] + core))
    return pairs


AHEAD = ring_pairs(1)
BEHIND = ring_pairs(-1)


def shape(dims, dtype=BF16):
    return jax.ShapeDtypeStruct(dims, dtype)


def call(
    body, ids, arrays, grid, ins, outs, shapes, scratch=(), after=(), aliases=None
):
    count = len(arrays)

    def kernel(ids_ref, *refs):
        body(ids_ref, *refs[:count], *refs[count + len(after) :])

    return pl.pallas_call(
        kernel,
        grid_spec=pltpu.PrefetchScalarGridSpec(
            num_scalar_prefetch=1,
            grid=grid,
            in_specs=list(ins) + [ANY] * len(after),
            out_specs=outs,
            scratch_shapes=scratch,
        ),
        out_shape=shapes,
        compiler_params=PARAMS,
        cost_estimate=WORK if grid else HINT,
        input_output_aliases=aliases or {},
    )(ids, *arrays, *after)


def later(ids, array, after):
    return call(
        lambda *refs: None, ids, [array], (), [ANY], ANY, shape(array.shape, array.dtype),
        after=after, aliases={1: 0},
    )


def whole(dims):
    return pl.BlockSpec(dims, lambda *_: (0,) * len(dims))


def make_ids():
    table = np.zeros((8, 4, 9), np.int32)
    for row in range(8):
        place, sense = CHIPS.index(row // 2), 1 - 2 * (row % 2)
        ring = [CHIPS[(place + sense * step) % 4] for step in (0, -1, 1, 2)]
        for z in range(4):
            table[row, z] = [z, (z + 1) % 4, (z + 2) % 4, (z + 3) % 4, row % 2] + ring
    place = (lax.axis_index("row"), lax.axis_index("col"), 0)
    return lax.dynamic_slice(jnp.asarray(table), place, (1, 1, 9)).reshape(9)


def move(body, ids, arrays, shapes, count, after=()):
    def kernel(ids_ref, *refs):
        sems = refs[-1]
        pairs = list(body(ids_ref, refs[: len(arrays)], refs[len(arrays) : -1]))
        copies = [pltpu.make_async_copy(src, dst, sems.at[i]) for i, (_, src, dst) in enumerate(pairs)]
        for (when, _, _), copy in zip(pairs, copies):
            if when is None:
                copy.start()
            else:
                pl.when(when)(copy.start)
        for (when, _, _), copy in zip(pairs, copies):
            if when is None:
                copy.wait()
            else:
                pl.when(when)(copy.wait)

    return call(
        kernel, ids, arrays, (), [ANY] * len(arrays), [VMEM] * len(shapes), shapes,
        [pltpu.SemaphoreType.DMA((count,))], after,
    )


def start_of(index, size):
    return pl.ds(pl.multiple_of(index * size, size), size)


def col_send(block):
    across = lax.ppermute(block, "col", ACROSS)
    above = lax.ppermute(block, "col", DOWN)
    below = lax.ppermute(block, "col", UP)
    return block, above, across, below


def col_gather(ids, parts, before_far):
    block, above, across, below = parts
    rows, cols = block.shape
    across = later(ids, across, before_far)
    far = lax.ppermute(across, "col", [(1, 0), (2, 3)])

    def body(i, s, t):
        def to(k):
            return t[0].at[:, start_of(i[k], cols)]

        z = i[0]
        yield None, s[0], to(0)
        yield None, s[2], to(2)
        yield z < 3, s[1], to(1)
        yield z == 3, s[4], to(1)
        yield z > 0, s[3], to(3)
        yield z == 0, s[4], to(3)

    return move(
        body, ids, [block, above, across, below, far], [shape((rows, 4 * cols))], 6
    )[0]


def normalize(ids, parts, scale, gains):
    rows, cols = scale.shape[0], parts[0].shape[1]

    def kernel(ids_ref, *refs):
        scale_ref, gain_ref, out_ref = refs[4:]
        inverse = scale_ref[:, 4:5]
        for k, place in enumerate((0, 3, 2, 1)):
            value = (refs[k][:rows].astype(F32) + scale_ref[:, k : k + 1]) * inverse
            value = value * gain_ref[k : k + 1]
            out_ref[:, start_of(ids_ref[place], cols)] = value.astype(BF16)

    return call(
        kernel, ids, [*parts, scale, gains], (), [VMEM] * 6, VMEM, shape((rows, 4 * cols))
    )


def gelu_parts(v):
    cdf = 0.5 * (1.0 + lax.erf(v * 0.7071067811865476))
    return v * cdf, cdf + v * jnp.exp(-0.5 * v * v) * 0.3989422804014327


TILE = 512


def expand(ids, rows, panel, after=()):
    hid = panel.shape[1] // 2
    steps = hid // TILE

    def kernel(ids_ref, x_ref, w_ref, hidden_ref, slope_ref):
        pre = jnp.dot(x_ref[...], w_ref[...], preferred_element_type=F32)
        act, slope = gelu_parts(pre)
        hidden_ref[...] = act.astype(BF16)
        slope_ref[...] = slope.astype(BF16)

    tile = pl.BlockSpec((rows.shape[0], TILE), lambda t, i: (0, t))
    return call(
        kernel, ids, [rows, panel], (steps,),
        [whole(rows.shape), pl.BlockSpec((C, TILE), lambda t, i: (0, i[4] * steps + t))],
        [tile, tile], [shape((rows.shape[0], hid))] * 2, after=after,
    )


def expand_grad(ids, strip, panel, slope, after):
    rows, hid = slope.shape
    steps = hid // TILE

    def kernel(ids_ref, x_ref, w_ref, slope_ref, out_ref):
        back = jnp.dot(x_ref[...], w_ref[...], preferred_element_type=F32)
        out_ref[...] = (back * slope_ref[...].astype(F32)).astype(BF16)

    tile = pl.BlockSpec((rows, TILE), lambda t, i: (0, t))
    return call(
        kernel, ids, [strip, panel, slope], (steps,),
        [
            whole(strip.shape),
            pl.BlockSpec((C, TILE), lambda t, i: (0, i[4] * steps + t)),
            tile,
        ],
        tile, shape((rows, hid)), after=after,
    )


def weight_grad(ids, own, sib, right, slots, after=()):
    rows = own.shape[0]
    hid = right[0].shape[1]
    size = C // 4

    def kernel(ids_ref, own_ref, sib_ref, own_right, sib_right, *outs):
        acc = lax.dot_general(own_ref[...], own_right[...], FIRST, preferred_element_type=F32)
        acc += lax.dot_general(sib_ref[...], sib_right[...], FIRST, preferred_element_type=F32)
        if not slots:
            outs[0][...] = acc.astype(BF16)
            return
        for k in range(4):
            @pl.when(pl.program_id(0) == k)
            def _():
                outs[k][...] = acc.astype(BF16)

    if slots:
        cut = pl.BlockSpec((rows, size), lambda t, i: (0, i[8 - t]))
        outs, shapes = [whole((size, hid))] * 4, [shape((size, hid))] * 4
    else:
        cut = pl.BlockSpec((rows, size), lambda t, i: (0, t))
        outs, shapes = pl.BlockSpec((size, hid), lambda t, i: (t, 0)), shape((C, hid))
    return call(
        kernel, ids, [own, sib, *right], (4,), [cut, cut] + [whole((rows, hid))] * 2, outs, shapes,
        after=after,
    )


def contract(ids, left, panel, other=None, after=()):
    rows, hid = left.shape

    def kernel(ids_ref, x_ref, w_ref, *refs):
        acc = lax.dot_general(x_ref[...], w_ref[...], LAST, preferred_element_type=F32)
        if other is not None:
            acc = acc + refs[0][...].astype(F32)
        refs[-1][...] = acc.astype(BF16)

    cut = pl.BlockSpec((rows, 1024), lambda t, i: (0, t))
    more = [] if other is None else [other]
    return call(
        kernel, ids, [left, panel, *more], (C // 1024,),
        [whole((rows, hid)), pl.BlockSpec((1024, hid), lambda t, i: (t, i[4]))] + [cut] * len(more),
        cut, shape((rows, C)), after=after,
    )


def contract_own(ids, left, panel, other, after=()):
    rows, hid = left.shape

    def kernel(ids_ref, x_ref, w_ref, o_ref, *outs):
        acc = lax.dot_general(x_ref[...], w_ref[...], LAST, preferred_element_type=F32)
        acc = (acc + o_ref[...].astype(F32)).astype(BF16)
        for k in range(4):
            @pl.when(pl.program_id(0) == k)
            def _():
                outs[k][...] = acc

    return call(
        kernel, ids, [left, panel, other], (4,),
        [
            whole((rows, hid)),
            pl.BlockSpec((512, hid), lambda t, i: (i[t], i[4])),
            pl.BlockSpec((rows, 512), lambda t, i: (0, i[t])),
        ],
        [whole((rows, 512))] * 4, [shape((rows, 512))] * 4, after=after,
    )


def ring_send(blocks):
    return lax.ppermute(blocks[0], "row", BEHIND), lax.ppermute(blocks[1], "row", AHEAD)


def ring_scatter(blocks, sent):
    _, _, behind, own = blocks
    one = lax.ppermute((sent[0].astype(F32) + behind.astype(F32)).astype(BF16), "row", BEHIND)
    return (own.astype(F32) + one.astype(F32) + sent[1].astype(F32)).astype(BF16)


def give_rows(ids, block, after):
    rows, cols = block.shape

    def body(i, s, t):
        yield None, s[0].at[start_of(1 - i[4], rows // 2)], t[0]

    return move(body, ids, [block], [shape((rows // 2, cols))], 1, after)[0]


def own_rows(ids, block, after=()):
    rows, cols = block.shape
    other = lax.ppermute(give_rows(ids, block, after), "row", SIBLING)

    def body(i, s, t):
        yield None, s[0].at[start_of(i[4], rows // 2)], t[0].at[:, start_of(i[4], cols)]
        yield None, s[1], t[0].at[:, start_of(1 - i[4], cols)]

    return move(body, ids, [block, other], [shape((rows // 2, 2 * cols))], 2)[0]


def taps(ids, low, mid, high, dw_kernel, flipped, extra=None, after=()):
    images, rows, width, chans = mid.shape
    lanes = 128
    edge = 8

    def kernel(ids_ref, *refs):
        low_ref, mid_ref, high_ref, dw_ref = refs[:4]
        outs, pad_ref = refs[4 + (extra is not None) : -1], refs[-1]
        pad_ref[:, :edge] = jnp.zeros((rows + 2 * REACH, edge, lanes), F32)
        pad_ref[:, edge + width :] = jnp.zeros((rows + 2 * REACH, edge, lanes), F32)

        @pl.loop(0, chans // lanes)
        def _(chunk):
            lane = start_of(chunk, lanes)
            pad_ref[:REACH, edge : edge + width] = low_ref[0, :, :, lane].astype(F32)
            pad_ref[REACH : REACH + rows, edge : edge + width] = mid_ref[0, :, :, lane].astype(F32)
            pad_ref[REACH + rows :, edge : edge + width] = high_ref[0, :, :, lane].astype(F32)
            totals = [jnp.zeros((width, lanes), F32)] * rows
            for off_col in range(KS):
                tap_col = KS - 1 - off_col if flipped else off_col
                for place in range(rows + 2 * REACH):
                    line = pad_ref[place, pl.ds(edge - REACH + off_col, width)]
                    for row in range(rows):
                        off_row = place - row
                        if 0 <= off_row < KS:
                            tap_row = KS - 1 - off_row if flipped else off_row
                            totals[row] += dw_ref[pl.ds(tap_row * KS + tap_col, 1), lane] * line
            for row in range(rows):
                if extra is None:
                    outs[0][0, row, :, lane] = totals[row]
                else:
                    total = refs[4][0, row, :, lane].astype(F32) + totals[row]
                    outs[0][0, row, :, lane] = total.astype(BF16)

        if extra is None:
            for row in range(rows):
                value = outs[0][0, row]
                mean = jnp.sum(value, axis=1, keepdims=True) * (1.0 / chans)
                value = value - mean
                outs[0][0, row] = value
                outs[1][0, row] = value.astype(BF16)
                outs[2][0, row] = mean
                outs[3][0, row] = jnp.sum(value * value, axis=1, keepdims=True)

    def strip(count, last=chans):
        return pl.BlockSpec((1, count, width, last), lambda b, i: (b, 0, 0, 0))

    arrays = [low, mid, high, dw_kernel.reshape(KS * KS, chans)]
    ins = [strip(REACH), strip(rows), strip(REACH), whole((KS * KS, chans))]
    if extra is None:
        thin = shape((images, rows, width, 1), F32)
        outs = [strip(rows), strip(rows), strip(rows, 1), strip(rows, 1)]
        shapes = [shape(mid.shape, F32), shape(mid.shape), thin, thin]
    else:
        arrays.append(extra)
        ins.append(strip(rows))
        outs, shapes = strip(rows), shape(mid.shape)
    return call(
        kernel, ids, arrays, (images,), ins, outs, shapes,
        [pltpu.VMEM((rows + 2 * REACH, width + 2 * edge, lanes), F32)], after,
    )


def rims(block):
    count = lax.axis_size("row")
    forward = [(i, i + 1) for i in range(count - 1)]
    backward = [(i + 1, i) for i in range(count - 1)]
    low = lax.ppermute(block[:, -REACH:], "row", forward)
    high = lax.ppermute(block[:, :REACH], "row", backward)
    return low, high


def split(row):
    high = lax.reduce_precision(row, 8, 7)
    mid = lax.reduce_precision(row - high, 8, 7)
    return [part.astype(BF16) for part in (high, mid, row - high - mid)]


def joined(rows):
    return rows[0].astype(F32) + rows[1].astype(F32) + rows[2].astype(F32)


def shifted(array, step):
    count = lax.axis_size("col")
    return lax.ppermute(array, "col", [(i, (i + step) % count) for i in range(count)])


def residual(ids, images, layer_scale, branch, after):
    rows, chans = images.shape

    def kernel(ids_ref, images_ref, scale_ref, branch_ref, out_ref):
        value = images_ref[...].astype(F32) + scale_ref[...] * branch_ref[...].astype(F32)
        out_ref[...] = value.astype(BF16)

    cut = pl.BlockSpec((rows // 2, chans), lambda t, i: (t, 0))
    return call(
        kernel, ids, [images, layer_scale.reshape(1, chans), branch], (2,),
        [cut, whole((1, chans)), cut], cut, shape((rows, chans)), after=after,
    )


def added(blocks):
    total = blocks[0].astype(F32)
    for block in blocks[1:]:
        total = total + block.astype(F32)
    return total


def row_scatter(whole_rows):
    return lax.psum_scatter(
        whole_rows, "row", scatter_dimension=0, tiled=True, axis_index_groups=SAME_CORE
    )


def on_device(images, dw_kernel, norm_gain, proj_in, proj_out, layer_scale, cotangent):
    local_ch = images.shape[3]
    pixels = images.shape[0] * images.shape[1] * images.shape[2]
    ids = make_ids()

    def swap(block):
        return lax.ppermute(block, "row", SIBLING)

    in_panel = lax.all_gather(proj_in, "row", axis=0, tiled=True)
    out_panel = lax.all_gather(proj_out, "row", axis=0, tiled=True)
    cot_flat = cotangent.reshape(pixels, local_ch).astype(F32)
    grad_branch = (cot_flat * layer_scale).astype(BF16)
    grad_parts = col_send(grad_branch)
    low, high = rims(images)
    centred, rounded, own_mean, own_square = taps(
        ids, low, images, high, dw_kernel, False, after=[grad_parts[1], grad_parts[3]]
    )
    centred = centred.reshape(pixels, local_ch)
    stats = [own_mean.reshape(pixels), own_square.reshape(pixels), norm_gain]
    extra = jnp.stack(split(stats[0]) + split(stats[1]) + split(stats[2]))
    extra = jnp.pad(extra, ((0, 16 - extra.shape[0]), (0, 0)))
    rounded = jnp.concatenate([rounded.reshape(pixels, local_ch), extra])
    parts = [rounded] + [shifted(rounded, step) for step in (1, 2, 3)]
    grad_own = col_gather(ids, grad_parts, before_far=[rounded])
    grad_sib = swap(grad_own)

    means, squares, gains = (
        jnp.stack([stats[k]] + [joined(part[pixels + 3 * k :]) for part in parts[1:]])
        for k in range(3)
    )
    row_mean = jnp.mean(means, axis=0)
    shifts = means - row_mean
    squares = squares + local_ch * (shifts * shifts)
    inv_std = lax.rsqrt(jnp.sum(squares, axis=0) / C + 1e-06)
    scale = jnp.concatenate([shifts, inv_std[None]]).T
    normed = (centred + shifts[0][:, None]) * inv_std[:, None]
    in_own = normalize(ids, parts, later(ids, scale, [grad_own]), gains)
    in_sib = swap(in_own)

    hidden_own, slope_own = expand(ids, in_own, in_panel)
    hidden_sib, slope_sib = expand(ids, in_sib, in_panel, [hidden_own])
    hidden = hidden_own, hidden_sib
    out_part = weight_grad(ids, grad_own, grad_sib, hidden, False)
    out_rows = row_scatter(out_part)
    pre_sib = expand_grad(ids, grad_sib, out_panel, slope_sib, [out_part])
    back_give = contract(ids, pre_sib, in_panel)
    back_sib = swap(back_give)
    pre_own = expand_grad(ids, grad_own, out_panel, slope_own, [back_give])
    back = contract_own(ids, pre_own, in_panel, back_sib)
    back_sent = [shifted(back[step], step) for step in (1, 2, 3)]
    branch_give = contract(ids, hidden_sib, out_panel, None, [back[0]])
    branch_sib = swap(branch_give)
    contrib = contract(ids, hidden_own, out_panel, branch_sib, [back[0]])
    in_parts = weight_grad(ids, in_own, in_sib, (pre_own, pre_sib), True, [contrib])
    in_sent = ring_send(in_parts)
    back_sent[0] = later(ids, back_sent[0], [in_parts[0], *back_sent[1:]])
    contrib = later(ids, contrib, [back_sent[0]])
    branch = lax.psum_scatter(contrib, "col", scatter_dimension=1, tiled=True)
    in_rows = ring_scatter(in_parts, in_sent)
    seen = back_sent[0][:8, :128] + back_sent[0][8:16, :128]
    back_sent[0] = later(ids, back_sent[0], [seen, *in_sent])
    grad_scaled = added([back[0], *back_sent])
    weighted = grad_scaled * norm_gain
    sums = jnp.stack([jnp.sum(weighted, axis=1), jnp.sum(weighted * normed, axis=1)])
    sums = sums + shifted(sums, 1) + shifted(sums, 2) + shifted(sums, 3)
    grad_conv = inv_std[:, None] * (
        weighted - sums[0][:, None] / C - normed * sums[1][:, None] / C
    )
    grad_conv = grad_conv.astype(BF16).reshape(images.shape)
    low, high = rims(grad_conv)
    grad_out = own_rows(ids, out_rows)
    grad_images = taps(
        ids, low, grad_conv, high, dw_kernel, True, cotangent, after=[grad_out]
    )
    grad_in = own_rows(ids, in_rows, [grad_images])
    flat = images.reshape(pixels, local_ch)
    block_out = residual(ids, flat, layer_scale, branch, [grad_in, grad_out]).reshape(images.shape)
    return block_out, grad_images, grad_in, grad_out


def with_halo(block, sides, width):
    for axis, dim in sides:
        count = lax.axis_size(axis)
        forward = [(i, i + 1) for i in range(count - 1)]
        backward = [(target, source) for source, target in forward]
        low = lax.ppermute(
            lax.slice_in_dim(block, block.shape[dim] - width, None, axis=dim), axis, forward
        )
        high = lax.ppermute(lax.slice_in_dim(block, 0, width, axis=dim), axis, backward)
        block = jnp.concatenate([low, block, high], axis=dim)
    return block


def taps_sum(padded, dw_kernel, img_rows, img_cols, flipped):
    total = jnp.zeros(padded.shape[:1] + (img_rows, img_cols) + padded.shape[3:], jnp.float32)
    reach = 2 * (KS // 2)
    for tap_row in range(KS):
        for tap_col in range(KS):
            off_row = reach - tap_row if flipped else tap_row
            off_col = reach - tap_col if flipped else tap_col
            total = (
                total
                + dw_kernel[tap_row, tap_col]
                * padded[:, off_row : off_row + img_rows, off_col : off_col + img_cols, :]
            )
    return total


def gelu_slope(values):
    return (
        0.5 * (1.0 + lax.erf(values * 0.7071067811865476))
        + values * jnp.exp(-0.5 * values * values) * 0.3989422804014327
    )


def on_any_mesh(images, dw_kernel, norm_gain, proj_in, proj_out, layer_scale, cotangent):
    img_batch, strip_rows, img_cols, local_ch = images.shape
    pixels = img_batch * strip_rows * img_cols
    reach = KS // 2
    contract_last = (((1,), (1,)), ((), ()))
    contract_first = (((0,), (0,)), ((), ()))
    rimmed = with_halo(images, (("row", 1),), reach)
    padded = jnp.pad(rimmed.astype(jnp.float32), ((0, 0), (0, 0), (reach, reach), (0, 0)))
    conv_out = taps_sum(padded, dw_kernel, strip_rows, img_cols, False).reshape(pixels, local_ch)
    row_mean = lax.psum(jnp.sum(conv_out, axis=1), "col") / C
    centred = conv_out - row_mean[:, None]
    row_var = lax.psum(jnp.sum(centred * centred, axis=1), "col") / C
    inv_std = lax.rsqrt(row_var + 1e-06)
    normed = centred * inv_std[:, None]
    scaled = (normed * norm_gain).astype(jnp.bfloat16)
    full_in = lax.all_gather(scaled, "col", axis=1, tiled=True)
    in_panel = lax.all_gather(proj_in, "row", axis=0, tiled=True)
    out_panel = lax.all_gather(proj_out, "row", axis=0, tiled=True)
    hidden_pre = jnp.dot(full_in, in_panel, preferred_element_type=jnp.float32)
    hidden = jax.nn.gelu(hidden_pre, approximate=False).astype(jnp.bfloat16)
    contrib = lax.dot_general(hidden, out_panel, contract_last, preferred_element_type=jnp.float32)
    branch = lax.psum_scatter(
        contrib.astype(jnp.bfloat16), "col", scatter_dimension=1, tiled=True
    ).astype(jnp.float32)
    residual_in = images.reshape(pixels, local_ch).astype(jnp.float32)
    block_out = (residual_in + layer_scale * branch.astype(F32)).astype(jnp.bfloat16).reshape(images.shape)
    cot_flat = cotangent.reshape(pixels, local_ch).astype(jnp.float32)
    grad_branch = (cot_flat * layer_scale).astype(jnp.bfloat16)
    full_grad = lax.all_gather(grad_branch, "col", axis=1, tiled=True)
    grad_proj_out = lax.psum_scatter(
        lax.dot_general(
            full_grad, hidden, contract_first, preferred_element_type=jnp.float32
        ).astype(jnp.bfloat16),
        "row",
        scatter_dimension=0,
        tiled=True,
    )
    grad_hidden = jnp.dot(full_grad, out_panel, preferred_element_type=jnp.float32)
    grad_pre = (grad_hidden * gelu_slope(hidden_pre)).astype(jnp.bfloat16)
    grad_proj_in = lax.psum_scatter(
        lax.dot_general(
            full_in, grad_pre, contract_first, preferred_element_type=jnp.float32
        ).astype(jnp.bfloat16),
        "row",
        scatter_dimension=0,
        tiled=True,
    )
    back_part = lax.dot_general(
        grad_pre, in_panel, contract_last, preferred_element_type=jnp.float32
    )
    grad_scaled = lax.psum_scatter(
        back_part.astype(jnp.bfloat16), "col", scatter_dimension=1, tiled=True
    ).astype(jnp.float32)
    weighted = grad_scaled * norm_gain
    sum_one, sum_two = lax.psum(
        (jnp.sum(weighted, axis=1), jnp.sum(weighted * normed, axis=1)), "col"
    )
    grad_conv = inv_std[:, None] * (weighted - sum_one[:, None] / C - normed * sum_two[:, None] / C)
    grad_conv = grad_conv.reshape(img_batch, strip_rows, img_cols, local_ch)
    grad_rim = with_halo(grad_conv.astype(jnp.bfloat16), (("row", 1),), reach).astype(
        grad_conv.dtype
    )
    grad_pad = jnp.pad(grad_rim, ((0, 0), (0, 0), (reach, reach), (0, 0)))
    input_grad = taps_sum(grad_pad, dw_kernel, strip_rows, img_cols, True)
    grad_images = (cotangent.astype(jnp.float32) + input_grad).astype(jnp.bfloat16)
    return (block_out, grad_images, grad_proj_in, grad_proj_out)


def solution(mesh):
    tuned = mesh.shape["row"] == 8 and mesh.shape["col"] == 4
    placed = (
        P(None, "row", None, "col"),
        P(None, None, "col"),
        P("col"),
        P("row", "col"),
        P("row", "col"),
        P("col"),
        P(None, "row", None, "col"),
    )
    return jax.shard_map(
        on_device if tuned else on_any_mesh,
        mesh=mesh,
        in_specs=placed,
        out_specs=(
            P(None, "row", None, "col"),
            P(None, "row", None, "col"),
            P("row", "col"),
            P("row", "col"),
        ),
        check_vma=False,
    )
```
